32 devices in a mesh: groups: 2 (over x), expert: 16 (over z, y, core).
Axes of the slice: x: 2, y: 2, z: 4, core: 2. Of those that a mesh axis runs over, the one named last changes fastest.
Arguments:
- tokens: bfloat16 [4096, 5120], P(('groups', 'expert')), parts along dimension 0, may hold values from -40 to 40
- expert_ids: int32 [4096], P(('groups', 'expert')), parts along dimension 0, may hold values from 0 to 127, as said below
- norm_gain: float32 [5120], replicated, may hold values from 0.1 to 1.9
- router: bfloat16 [5120, 8], replicated, may hold values from -0.078125 to 0.078125
- gate_weight: bfloat16 [5120, 40960], P(None, 'expert'), may hold values from -0.078125 to 0.078125
- up_weight: bfloat16 [5120, 40960], P(None, 'expert'), may hold values from -0.078125 to 0.078125
- down_weight: bfloat16 [40960, 5120], P('expert'), may hold values from -0.3125 to 0.3125
Outputs:
- routed: bfloat16 [4096, 5120], P(('groups', 'expert')), parts along dimension 0
The draws below stay inside these ranges and needn't reach their ends.
There are 2 independent parts, one for each index of `groups`. The reference program is written for one: setup_inputs(seed, part) draws one part's arguments, and reference() takes and returns one part's arrays. A program takes and returns all parts, laid end to end along the dimension named above; an argument that names none is the same for every part. Nothing has to cross between parts.
Inputs may be any that keep to these rules, and one draw needn't show every extreme that they name: `expert_ids`: among one device's 128 tokens at most 4 name any one expert below 8, and exactly 4 of them name one such expert, the same one for every device.
All inputs are finite; a program needn't handle non-finite values.
Results may differ from the reference program's by a relative error of at most 0.019.
Values may be sent and summed in bfloat16 or wider, within the bound.
No kernel may reach another device: no remote copies, remote signals or barrier semaphores. Data moves between devices by JAX's collectives and lax.ppermute only.
A program may use at most 192 MiB of HBM per device.

```python
import jax
import jax.numpy as jnp
from jax import lax

MODEL_DIM = 5120
HID_WIN = 5120
EXPERTS = 128
EXP_FL = 8
DEVICE_TOKENS = 128
CAP = 4
TOKENS = 2048
N_EXPERT = 16


def draw_tokens(key, part):
    key = jax.random.fold_in(key, 3)
    key_base, key_cols, key_rows = jax.random.split(key, 3)
    columns = jnp.exp(jax.random.uniform(key_cols, (1, MODEL_DIM), jnp.float32, -1.15, 1.15))
    rowscale = jnp.exp(jax.random.uniform(key_rows, (TOKENS, 1), jnp.float32, -1.15, 1.15))
    base = jnp.clip(jax.random.normal(key_base, (TOKENS, MODEL_DIM), jnp.float32), -4.0, 4.0)
    return (base * columns * rowscale).astype(jnp.bfloat16)


def draw_expert_ids(key, part):
    key = jax.random.fold_in(key, 7)
    key_busy, key_active, key_other, key_order = jax.random.split(key, 4)
    block_list = TOKENS // DEVICE_TOKENS
    block_span = EXP_FL * CAP
    busiest = jax.random.randint(key_busy, (), 0, EXP_FL)
    rank_grid = jnp.arange(DEVICE_TOKENS, dtype=jnp.int32)[None, :]
    active_rows = jax.random.randint(key_active, (block_list, DEVICE_TOKENS), 0, 5) < 2
    active_rows = active_rows | (rank_grid < CAP)
    inside = (busiest + rank_grid // CAP) % EXP_FL
    outside = jax.random.randint(key_other, (block_list, DEVICE_TOKENS), EXP_FL, EXPERTS)
    outside = outside.at[0, DEVICE_TOKENS - 1].set(EXPERTS - 1)
    by_rank = jnp.where((rank_grid < block_span) & active_rows, inside, outside)
    orders = jax.vmap(lambda single: jax.random.permutation(single, DEVICE_TOKENS))(jax.random.split(key_order, block_list))
    chosen = jnp.take_along_axis(by_rank, orders, axis=1)
    return chosen.reshape(TOKENS).astype(jnp.int32)


def level_of(own_key, shape, shards, low, high):
    def one(dim, shards_of):
        steps = jax.random.uniform(jax.random.fold_in(jax.random.fold_in(own_key, 6), dim), (shards_of,), jnp.float32, low / len(shards), high / len(shards))
        return jnp.repeat(jnp.exp(steps), shape[dim] // shards_of).reshape((-1,) + (1,) * (len(shape) - dim - 1))

    level = one(*shards[0])
    for cut in shards[1:]:
        level = level * one(*cut)
    return level


def gaussian(stream_key, dims, width, bound, cuts=(), held_as=jnp.bfloat16):
    level = level_of(stream_key, dims, cuts, -0.22, 0.18) if cuts else 1.0
    entries = jax.random.normal(stream_key, dims, jnp.float32) * width * level
    return jnp.minimum(jnp.maximum(entries, -bound), bound).astype(held_as)


def setup_inputs(seed: int = 0, part: int = 0) -> dict:
    splits = jax.random.split(jax.random.key(seed), 8)
    part_splits = jax.random.split(jax.random.fold_in(splits[7], part), 8)
    tokens = draw_tokens(jax.random.fold_in(jax.random.fold_in(splits[7], part), 71), part)
    expert_ids = draw_expert_ids(jax.random.fold_in(jax.random.fold_in(splits[7], part), 71), part)
    norm_gain = jnp.clip(1.0 + 0.18 * jax.random.normal(splits[2], (MODEL_DIM,), jnp.float32), 0.1, 1.9)
    router = gaussian(splits[3], (MODEL_DIM, EXP_FL), MODEL_DIM ** -0.5, 0.078125)
    gate_weight = gaussian(splits[4], (MODEL_DIM, EXP_FL * HID_WIN), MODEL_DIM ** -0.5, 0.078125, ((1, 16),))
    up_weight = gaussian(splits[5], (MODEL_DIM, EXP_FL * HID_WIN), MODEL_DIM ** -0.5, 0.078125, ((1, 16),))
    down_weight = gaussian(splits[6], (EXP_FL * HID_WIN, MODEL_DIM), (HID_WIN // 16) ** -0.5, 0.3125, ((0, 16),))
    return {"tokens": tokens, "expert_ids": expert_ids, "norm_gain": norm_gain, "router": router, "gate_weight": gate_weight, "up_weight": up_weight, "down_weight": down_weight}


def reference(tokens, expert_ids, norm_gain, router, gate_weight, up_weight, down_weight):
    split_count = N_EXPERT // EXP_FL
    slice_width = HID_WIN // split_count
    hidden_state = tokens.astype(jnp.float32)
    mean_square = lax.optimization_barrier(jnp.mean(hidden_state * hidden_state, axis=-1, keepdims=True))
    normed = (hidden_state * lax.rsqrt(mean_square + 1e-05) * norm_gain).astype(jnp.bfloat16)
    logits = jnp.dot(normed, router, preferred_element_type=jnp.float32)
    chosen = expert_ids[:, None] == jnp.arange(EXP_FL, dtype=jnp.int32)[None, :]
    gate_score = jax.nn.sigmoid(lax.optimization_barrier(jnp.sum(jnp.where(chosen, logits, 0.0), axis=-1)))
    routed_input = (normed.astype(jnp.float32) * gate_score[:, None]).astype(jnp.bfloat16)
    block_list = TOKENS // DEVICE_TOKENS
    chosen_int = chosen.astype(jnp.int32).reshape(block_list, DEVICE_TOKENS, EXP_FL)
    earlier = jnp.cumsum(chosen_int, axis=1) - chosen_int
    slot_index = lax.optimization_barrier(jnp.sum(earlier * chosen_int, axis=-1)).astype(jnp.int32)
    ids_block = expert_ids.reshape(block_list, DEVICE_TOKENS)
    target = jnp.where(ids_block < EXP_FL, ids_block * CAP + slot_index, -1).astype(jnp.int32)
    slot_grid = jnp.arange(EXP_FL * CAP, dtype=jnp.int32)
    block_layout = (slot_grid[None, :, None] == target[:, None, :]).astype(jnp.float32)
    buffer_list = jnp.einsum('ryi,rim->rym', block_layout, routed_input.astype(jnp.float32).reshape(block_list, DEVICE_TOKENS, MODEL_DIM), precision=lax.Precision.HIGHEST).astype(jnp.bfloat16)
    per_expert = buffer_list.reshape(block_list, EXP_FL, CAP, MODEL_DIM).transpose(1, 0, 2, 3).reshape(EXP_FL, block_list * CAP, MODEL_DIM)
    gate_all = gate_weight.reshape(MODEL_DIM, EXP_FL, HID_WIN).transpose(1, 0, 2)
    up_all = up_weight.reshape(MODEL_DIM, EXP_FL, HID_WIN).transpose(1, 0, 2)
    down_all = down_weight.reshape(EXP_FL, split_count, slice_width, MODEL_DIM)

    def expert_out(inputs):
        slot_rows, w_gate, w_up, w_down = inputs
        gate_out = jnp.dot(slot_rows, w_gate, preferred_element_type=jnp.float32)
        up_out = jnp.dot(slot_rows, w_up, preferred_element_type=jnp.float32)
        hidden = (jax.nn.silu(gate_out) * up_out).astype(jnp.bfloat16)
        pieces = hidden.reshape(slot_rows.shape[0], split_count, slice_width)
        partial_value = jnp.einsum('rsh,shd->srd', pieces.astype(jnp.float32), w_down.astype(jnp.float32)).astype(jnp.bfloat16)
        partial_value = lax.optimization_barrier(partial_value)
        return lax.optimization_barrier(jnp.sum(partial_value.astype(jnp.float32), axis=0)).astype(jnp.bfloat16)
    outputs = lax.map(expert_out, (per_expert, gate_all, up_all, down_all))
    outputs = lax.optimization_barrier(outputs).astype(jnp.float32)
    block_share = outputs.reshape(EXP_FL, block_list, CAP, MODEL_DIM).transpose(1, 0, 2, 3).reshape(block_list, EXP_FL * CAP, MODEL_DIM)
    routed = jnp.einsum('rnl,rnj->rlj', block_layout, block_share, precision=lax.Precision.HIGHEST)
    return routed.reshape(TOKENS, MODEL_DIM).astype(jnp.bfloat16)
```

```python
import functools

import jax
import jax.numpy as jnp
from jax import lax
from jax.experimental import pallas as pl
from jax.experimental.pallas import tpu as pltpu
from jax.sharding import PartitionSpec as P

EXP_FL = 8
CAP = 4
MIB = 1 << 20


def slot_layout(ids, rows):
    tokens = ids.shape[1]
    expert = lax.broadcasted_iota(jnp.int32, (EXP_FL, tokens), 0)
    chosen = (jnp.broadcast_to(ids, (EXP_FL, tokens)) == expert).astype(jnp.float32)
    before = lax.broadcasted_iota(jnp.int32, (tokens, tokens), 0) < lax.broadcasted_iota(
        jnp.int32, (tokens, tokens), 1
    )
    earlier = jnp.dot(
        chosen.astype(jnp.bfloat16),
        before.astype(jnp.float32).astype(jnp.bfloat16),
        preferred_element_type=jnp.float32,
    )
    slot = jnp.sum(earlier * chosen, axis=0, keepdims=True).astype(jnp.int32)
    target = jnp.where(ids < EXP_FL, ids * CAP + slot, -1)
    row = lax.broadcasted_iota(jnp.int32, (rows, tokens), 0)
    return (row == jnp.broadcast_to(target, (rows, tokens))).astype(jnp.float32).astype(jnp.bfloat16)


def pack_kernel(ids_ref, tokens_ref, gain_ref, router_ref, out_ref):
    rows = out_ref.shape[0]
    layout = slot_layout(ids_ref[...], rows)
    packed = jnp.dot(layout, tokens_ref[...], preferred_element_type=jnp.float32)
    mean_square = jnp.mean(packed * packed, axis=-1, keepdims=True)
    normed = (packed * lax.rsqrt(mean_square + 1e-05) * gain_ref[...]).astype(jnp.bfloat16)
    logits = lax.dot_general(
        normed, router_ref[...], (((1,), (1,)), ((), ())), preferred_element_type=jnp.float32
    )
    own = lax.broadcasted_iota(jnp.int32, logits.shape, 0) // CAP == lax.broadcasted_iota(
        jnp.int32, logits.shape, 1
    )
    logit = jnp.sum(jnp.where(own, logits, 0.0), axis=-1, keepdims=True)
    out_ref[...] = (normed.astype(jnp.float32) * jax.nn.sigmoid(logit)).astype(jnp.bfloat16)


def pack(tokens, ids, gain, router_rows):
    return pl.pallas_call(
        pack_kernel,
        out_shape=jax.ShapeDtypeStruct((EXP_FL * CAP, tokens.shape[1]), jnp.bfloat16),
        compiler_params=pltpu.CompilerParams(vmem_limit_bytes=24 * MIB),
        name="pack",
    )(ids, tokens, gain, router_rows)


def fetch_kernel(weight_ref, out_ref, sems):
    count = sems.shape[0]
    part = weight_ref.shape[0] // count
    copies = [
        pltpu.make_async_copy(
            weight_ref.at[pl.ds(i * part, part)], out_ref.at[pl.ds(i * part, part)], sems.at[i]
        )
        for i in range(count)
    ]
    for copy in copies:
        copy.start()
    for copy in copies:
        copy.wait()


def in_hbm(x):
    return pltpu.with_memory_space_constraint(x, pltpu.HBM)


def fetch(weight):
    return pl.pallas_call(
        fetch_kernel,
        in_specs=[pl.BlockSpec(memory_space=pl.ANY)],
        out_specs=pl.BlockSpec(memory_space=pltpu.VMEM),
        out_shape=pltpu.VMEM(weight.shape, weight.dtype),
        scratch_shapes=[pltpu.SemaphoreType.DMA((4,))],
        compiler_params=pltpu.CompilerParams(vmem_limit_bytes=1 * MIB),
        cost_estimate=pl.CostEstimate(
            flops=0, bytes_accessed=2 * weight.size * weight.dtype.itemsize, transcendentals=0
        ),
        name="fetch",
    )(in_hbm(weight))


def ffn_kernel(
    deep, wide, x_ref, gate_ref, up_ref, down_ref, out_ref, sems, acc_a, acc_b, acc_c, hid, ring, *rings
):
    down_ring = rings[0] if rings else ring
    width = x_ref.shape[1]
    units = gate_ref.shape[1]
    slots = ring.shape[0]
    ups = width // deep
    down_deep = min(deep, units)
    downs_k = units // down_deep
    halves = width // wide
    total = ups + halves * downs_k

    def up_copy(i):
        slot = lax.rem(i, slots)
        row = pl.multiple_of(i * deep, deep)
        return pltpu.make_async_copy(
            up_ref.at[pl.ds(row, deep)], ring.at[slot], sems.at[slot]
        )

    def down_copy(i):
        slot = lax.rem(i, slots)
        j = i - ups
        row = pl.multiple_of(lax.rem(j, downs_k) * down_deep, down_deep)
        col = pl.multiple_of((j // downs_k) * wide, wide)
        return pltpu.make_async_copy(
            down_ref.at[pl.ds(row, down_deep), pl.ds(col, wide)],
            down_ring.at[slot],
            sems.at[slot],
        )

    def start(i):
        @pl.when(i < ups)
        def _():
            up_copy(i).start()

        @pl.when(jnp.logical_and(i >= ups, i < total))
        def _():
            down_copy(i).start()

    @pl.loop(0, min(slots, total))
    def _(i):
        start(i)

    acc_a[...] = jnp.zeros_like(acc_a)
    acc_b[...] = jnp.zeros_like(acc_b)

    @pl.loop(0, ups)
    def _(i):
        row = pl.multiple_of(i * deep, deep)
        acc_a[...] += jnp.dot(
            x_ref[:, pl.ds(row, deep)],
            gate_ref[pl.ds(row, deep), :],
            preferred_element_type=jnp.float32,
        )

    @pl.loop(0, ups)
    def _(i):
        slot = lax.rem(i, slots)
        row = pl.multiple_of(i * deep, deep)
        up_copy(i).wait()
        acc_b[...] += jnp.dot(
            x_ref[:, pl.ds(row, deep)],
            ring[slot],
            preferred_element_type=jnp.float32,
        )
        start(i + slots)

    gate = acc_a[...]
    hid[...] = (gate / (1.0 + jnp.exp(-gate)) * acc_b[...]).astype(jnp.bfloat16)

    for half in range(halves):
        acc_c[...] = jnp.zeros_like(acc_c)

        @pl.loop(0, downs_k)
        def _(k, half=half):
            i = ups + half * downs_k + k
            slot = lax.rem(i, slots)
            down_copy(i).wait()
            row = pl.multiple_of(k * down_deep, down_deep)
            acc_c[...] += jnp.dot(
                hid[:, pl.ds(row, down_deep)] if downs_k > 1 else hid[...],
                down_ring[slot],
                preferred_element_type=jnp.float32,
            )
            start(i + slots)

        out_ref[:, half * wide : (half + 1) * wide] = acc_c[...].astype(jnp.bfloat16)


def ffn(x, gate, up, down):
    rows, width = x.shape
    units = gate.shape[1]
    deep, wide = 512, width // 2
    slots = 11
    down_deep = min(deep, units)
    rings = [pltpu.VMEM((slots, deep, units), jnp.bfloat16)]
    if (down_deep, wide) != (deep, units):
        rings.append(pltpu.VMEM((slots, down_deep, wide), jnp.bfloat16))
    return pl.pallas_call(
        functools.partial(ffn_kernel, deep, wide),
        in_specs=[
            pl.BlockSpec(memory_space=pltpu.VMEM),
            pl.BlockSpec(memory_space=pltpu.VMEM),
            pl.BlockSpec(memory_space=pl.ANY),
            pl.BlockSpec(memory_space=pl.ANY),
        ],
        out_specs=pl.BlockSpec(memory_space=pltpu.VMEM),
        out_shape=jax.ShapeDtypeStruct((rows, width), jnp.bfloat16),
        scratch_shapes=[
            pltpu.SemaphoreType.DMA((slots,)),
            pltpu.VMEM((rows, units), jnp.float32),
            pltpu.VMEM((rows, units), jnp.float32),
            pltpu.VMEM((rows, wide), jnp.float32),
            pltpu.VMEM((rows, units), jnp.bfloat16),
            *rings,
        ],
        compiler_params=pltpu.CompilerParams(vmem_limit_bytes=(34 if rows <= 64 else 58) * MIB),
        cost_estimate=pl.CostEstimate(
            flops=6 * rows * width * units,
            bytes_accessed=4 * width * units,
            transcendentals=rows * units,
        ),
        name="ffn",
    )(x, pltpu.with_memory_space_constraint(gate, pltpu.VMEM), in_hbm(up), in_hbm(down))


def unpack_kernel(ids_ref, rows_ref, out_ref):
    layout = slot_layout(ids_ref[...], rows_ref.shape[0])
    out_ref[...] = lax.dot_general(
        layout, rows_ref[...], (((0,), (0,)), ((), ())), preferred_element_type=jnp.float32
    ).astype(jnp.bfloat16)


def unpack(rows, ids):
    return pl.pallas_call(
        unpack_kernel,
        out_shape=jax.ShapeDtypeStruct((ids.shape[1], rows.shape[1]), jnp.bfloat16),
        compiler_params=pltpu.CompilerParams(vmem_limit_bytes=24 * MIB),
        name="unpack",
    )(ids, rows)


def per_device(tokens, expert_ids, norm_gain, router, gate_weight, up_weight, down_weight):
    devices = lax.axis_size("expert")
    chips = devices // 2
    copies = chips // EXP_FL
    width = tokens.shape[1]
    same_core = [list(range(core, devices, 2)) for core in range(2)]
    sibling = [(i, i ^ 1) for i in range(devices)]
    ids = expert_ids.reshape(1, -1)

    packed = pack(tokens, ids, norm_gain.reshape(1, -1), router.T)
    outgoing = packed.reshape(EXP_FL, 1, CAP, width)
    if copies > 1:
        outgoing = jnp.broadcast_to(outgoing, (EXP_FL, copies, CAP, width))
    outgoing = outgoing.reshape(chips, CAP, width)
    mine = lax.all_to_all(
        outgoing, "expert", split_axis=0, concat_axis=0, tiled=True, axis_index_groups=same_core
    )
    gate = fetch(gate_weight)
    other = lax.ppermute(mine, "expert", sibling)
    x = jnp.concatenate([mine, other], axis=0).reshape(2 * chips * CAP, width)
    partial = ffn(x, gate, up_weight, down_weight)
    own, lent = partial[: chips * CAP], partial[chips * CAP :]
    back = lax.ppermute(lent, "expert", sibling)
    summed = (own.astype(jnp.float32) + back.astype(jnp.float32)).astype(jnp.bfloat16)
    returned = lax.all_to_all(
        summed.reshape(chips, CAP, width),
        "expert",
        split_axis=0,
        concat_axis=0,
        tiled=True,
        axis_index_groups=same_core,
    )
    if copies > 1:
        returned = jnp.sum(
            returned.reshape(EXP_FL, copies, CAP, width).astype(jnp.float32), axis=1
        ).astype(jnp.bfloat16)
    return unpack(returned.reshape(EXP_FL * CAP, width), ids)


def solution(mesh):
    in_specs = (
        P(("groups", "expert"), None),
        P(("groups", "expert")),
        P(),
        P(),
        P(None, "expert"),
        P(None, "expert"),
        P("expert", None),
    )
    out_specs = P(("groups", "expert"), None)
    return jax.shard_map(
        per_device, mesh=mesh, in_specs=in_specs, out_specs=out_specs, check_vma=False
    )
```

```python
import functools
import math

import jax
import jax.numpy as jnp
from jax import lax
from jax.experimental import pallas as pl
from jax.experimental.pallas import tpu as pltpu
from jax.sharding import PartitionSpec as P

EXP_FL = 8
CAP = 4
MIB = 1 << 20
DEEP = 512


def slot_layout(ids, experts):
    tokens = ids.shape[1]
    rows = experts.shape[0]
    expert = lax.broadcasted_iota(jnp.int32, (EXP_FL, tokens), 0)
    chosen = (jnp.broadcast_to(ids, (EXP_FL, tokens)) == expert).astype(jnp.float32)
    before = lax.broadcasted_iota(jnp.int32, (tokens, tokens), 0) < lax.broadcasted_iota(
        jnp.int32, (tokens, tokens), 1
    )
    earlier = jnp.dot(
        chosen.astype(jnp.bfloat16),
        before.astype(jnp.float32).astype(jnp.bfloat16),
        preferred_element_type=jnp.float32,
    )
    slot = jnp.sum(earlier * chosen, axis=0, keepdims=True).astype(jnp.int32)
    target = jnp.where(ids < EXP_FL, ids * CAP + slot, -1)
    row = experts * CAP + lax.broadcasted_iota(jnp.int32, (rows, 1), 0) % CAP
    return (row == jnp.broadcast_to(target, (rows, tokens))).astype(jnp.float32).astype(jnp.bfloat16)


def grid_of(chips):
    inner = 1 << (int(math.log2(chips)) // 2)
    return chips // inner, inner


def partner_chips(chips, index):
    outers, inners = grid_of(chips)
    here = lax.axis_index("expert") // 2
    return here ^ ((index % outers) * inners + index // outers)


def in_hbm(x):
    return pltpu.with_memory_space_constraint(x, pltpu.HBM)


def in_vmem(x):
    return pltpu.with_memory_space_constraint(x, pltpu.VMEM)


def blocks_in_vmem(x):
    return in_vmem(x) if x.size <= MIB else x


def blocks_out(shape):
    if math.prod(shape) <= MIB:
        return pltpu.VMEM(shape, jnp.bfloat16)
    return jax.ShapeDtypeStruct(shape, jnp.bfloat16)


def join_rows(blocks_ref, rows_ref, first):
    for i in range(blocks_ref.shape[0]):
        rows_ref[first + i * CAP : first + (i + 1) * CAP, :] = blocks_ref[i].astype(rows_ref.dtype)


def fetch_parts(weight_ref, first, out_ref, sems):
    depth = out_ref.shape[0] // sems.shape[0]
    return [
        pltpu.make_async_copy(
            weight_ref.at[pl.ds(first + i * depth, depth)],
            out_ref.at[pl.ds(i * depth, depth)],
            sems.at[i],
        )
        for i in range(sems.shape[0])
    ]


def pack_kernel(first, outers, *refs):
    ids_ref, tokens_ref, gain_ref, router_ref, weight_ref = refs[:5]
    outs, held_ref = refs[5:-7], refs[-7]
    ids, tokens, gain, router, sems, fetch_sems = refs[-6:]
    pairs = ((ids_ref, ids), (tokens_ref, tokens), (gain_ref, gain), (router_ref, router))
    moves = [pltpu.make_async_copy(a, b, sems.at[i]) for i, (a, b) in enumerate(pairs)]
    for move in moves:
        move.start()
    parts = fetch_parts(weight_ref, first, held_ref, fetch_sems)
    for part in parts:
        part.start()
    chips = outers * len(outs)
    rows = chips * CAP
    copies = chips // EXP_FL
    index = lax.broadcasted_iota(jnp.int32, (rows, 1), 0) // CAP
    experts = partner_chips(chips, index) // copies
    moves[0].wait()
    layout = slot_layout(ids[...], experts)
    moves[1].wait()
    packed = jnp.dot(layout, tokens[...], preferred_element_type=jnp.float32)
    mean_square = jnp.mean(packed * packed, axis=-1, keepdims=True)
    moves[2].wait()
    normed = (packed * lax.rsqrt(mean_square + 1e-05) * gain[...]).astype(jnp.bfloat16)
    moves[3].wait()
    logits = lax.dot_general(
        normed, router[...], (((1,), (1,)), ((), ())), preferred_element_type=jnp.float32
    )
    own = lax.broadcasted_iota(jnp.int32, logits.shape, 1) == experts
    logit = jnp.sum(jnp.where(own, logits, 0.0), axis=-1, keepdims=True)
    routed = normed.astype(jnp.float32) * jax.nn.sigmoid(logit)
    for i in range(chips):
        outs[i // outers][i % outers] = routed[i * CAP : (i + 1) * CAP].astype(jnp.bfloat16)
    for part in parts:
        part.wait()


def pack(tokens, ids, gain, router_rows, weight, chips, first, count):
    width = tokens.shape[1]
    units = weight.shape[1]
    outers, inners = grid_of(chips)
    arrays = (ids, tokens, gain, router_rows)
    vmem = pl.BlockSpec(memory_space=pltpu.VMEM)
    outs = pl.pallas_call(
        functools.partial(pack_kernel, first * DEEP, outers),
        in_specs=[pl.BlockSpec(memory_space=pl.ANY)] * 5,
        out_specs=[vmem] * (inners + 1),
        out_shape=[blocks_out((outers, CAP, width))] * inners
        + [pltpu.VMEM((count * DEEP, units), weight.dtype)],
        scratch_shapes=[pltpu.VMEM(x.shape, x.dtype) for x in arrays]
        + [pltpu.SemaphoreType.DMA((4,)), pltpu.SemaphoreType.DMA((count,))],
        compiler_params=pltpu.CompilerParams(vmem_limit_bytes=(12 if chips <= 8 else 40) * MIB),
        name="pack",
    )(*[in_hbm(x) for x in (*arrays, weight)])
    return outs[:-1], outs[-1]


def fetch_kernel(first, weight_ref, out_ref, sems):
    parts = fetch_parts(weight_ref, first, out_ref, sems)
    for part in parts:
        part.start()
    for part in parts:
        part.wait()


def fetch(weight, first, count):
    return pl.pallas_call(
        functools.partial(fetch_kernel, first * DEEP),
        in_specs=[pl.BlockSpec(memory_space=pl.ANY)],
        out_specs=pl.BlockSpec(memory_space=pltpu.VMEM),
        out_shape=pltpu.VMEM((count * DEEP, weight.shape[1]), weight.dtype),
        scratch_shapes=[pltpu.SemaphoreType.DMA((count,))],
        compiler_params=pltpu.CompilerParams(vmem_limit_bytes=1 * MIB),
        cost_estimate=pl.CostEstimate(
            flops=0,
            bytes_accessed=count * DEEP * weight.shape[1] * weight.dtype.itemsize,
            transcendentals=0,
        ),
        name="fetch",
    )(in_hbm(weight))


def regroup_kernel(first, groups, *refs):
    for i, out_ref in enumerate(refs[groups:]):
        for j in range(groups):
            out_ref[j] = refs[j][first + i]


def regroup(arrays, first):
    count, _, width = arrays[0].shape
    vmem = pl.BlockSpec(memory_space=pltpu.VMEM)
    return pl.pallas_call(
        functools.partial(regroup_kernel, first, len(arrays)),
        in_specs=[vmem] * len(arrays),
        out_specs=[vmem] * (count - first),
        out_shape=[blocks_out((len(arrays), CAP, width))] * (count - first),
        compiler_params=pltpu.CompilerParams(vmem_limit_bytes=(4 if count <= 8 else 24) * MIB),
        name="regroup",
    )(*[blocks_in_vmem(x) for x in arrays])


def gather_kernel(kept, *refs):
    out_ref = refs[-1]
    for i in range(kept):
        out_ref[i] = refs[i][0]
    for i, ref in enumerate(refs[kept:-1]):
        out_ref[(i + 1) * kept : (i + 2) * kept] = ref[...]


def gather(kept, arrived):
    arrays = (*kept, *arrived)
    _, _, width = kept[0].shape
    chips = len(kept) * (len(arrived) + 1)
    return pl.pallas_call(
        functools.partial(gather_kernel, len(kept)),
        in_specs=[pl.BlockSpec(memory_space=pltpu.VMEM)] * len(arrays),
        out_specs=pl.BlockSpec(memory_space=pltpu.VMEM),
        out_shape=blocks_out((chips, CAP, width)),
        compiler_params=pltpu.CompilerParams(vmem_limit_bytes=(4 if chips <= 8 else 24) * MIB),
        name="gather",
    )(*[blocks_in_vmem(x) for x in arrays])


def ffn_kernel(
    deep,
    wide,
    held,
    mine_ref,
    other_ref,
    gate_ref,
    up_ref,
    down_ref,
    *refs,
):
    held_refs, (own_ref, lent_ref, sems, x_ref, acc_a, acc_b, acc_c, hid, ring, *rings) = (
        refs[: len(held)],
        refs[len(held) :],
    )
    down_ring = rings[0] if rings else ring
    chips, _, width = mine_ref.shape
    units = gate_ref.shape[1]
    slots = ring.shape[0]
    chunks = width // deep
    gates = chunks - sum(held)
    ups = gates + chunks
    down_deep = min(deep, units)
    downs_k = units // down_deep
    halves = width // wide
    total = ups + halves * downs_k

    def gate_copy(i):
        slot = lax.rem(i, slots)
        row = pl.multiple_of((i + chunks - gates) * deep, deep)
        return pltpu.make_async_copy(gate_ref.at[pl.ds(row, deep)], ring.at[slot], sems.at[slot])

    def up_copy(i):
        slot = lax.rem(i, slots)
        row = pl.multiple_of((i - gates) * deep, deep)
        return pltpu.make_async_copy(up_ref.at[pl.ds(row, deep)], ring.at[slot], sems.at[slot])

    def down_copy(i):
        slot = lax.rem(i, slots)
        j = i - ups
        row = pl.multiple_of(lax.rem(j, downs_k) * down_deep, down_deep)
        col = pl.multiple_of((j // downs_k) * wide, wide)
        return pltpu.make_async_copy(
            down_ref.at[pl.ds(row, down_deep), pl.ds(col, wide)],
            down_ring.at[slot],
            sems.at[slot],
        )

    def start(i):
        @pl.when(i < gates)
        def _():
            gate_copy(i).start()

        @pl.when(jnp.logical_and(i >= gates, i < ups))
        def _():
            up_copy(i).start()

        @pl.when(jnp.logical_and(i >= ups, i < total))
        def _():
            down_copy(i).start()

    @pl.loop(0, min(slots, total))
    def _(i):
        start(i)

    join_rows(mine_ref, x_ref, 0)
    join_rows(other_ref, x_ref, chips * CAP)
    acc_a[...] = jnp.zeros_like(acc_a)
    acc_b[...] = jnp.zeros_like(acc_b)

    done = 0
    for held_ref, count in zip(held_refs, held):

        @pl.loop(0, count)
        def _(i, held_ref=held_ref, done=done):
            acc_a[...] += jnp.dot(
                x_ref[:, pl.ds(pl.multiple_of((done + i) * deep, deep), deep)],
                held_ref[pl.ds(pl.multiple_of(i * deep, deep), deep), :],
                preferred_element_type=jnp.float32,
            )

        done += count

    for acc, copy_of, begin, end, base in (
        (acc_a, gate_copy, 0, gates, done),
        (acc_b, up_copy, gates, ups, -gates),
    ):

        @pl.loop(begin, end)
        def _(i, acc=acc, copy_of=copy_of, base=base):
            copy_of(i).wait()
            acc[...] += jnp.dot(
                x_ref[:, pl.ds(pl.multiple_of((base + i) * deep, deep), deep)],
                ring[lax.rem(i, slots)],
                preferred_element_type=jnp.float32,
            )
            start(i + slots)

    gate = acc_a[...]
    hid[...] = (gate / (1.0 + jnp.exp(-gate)) * acc_b[...]).astype(jnp.bfloat16)

    for half in range(halves):
        acc_c[...] = jnp.zeros_like(acc_c)

        @pl.loop(0, downs_k)
        def _(k, half=half):
            i = ups + half * downs_k + k
            slot = lax.rem(i, slots)
            down_copy(i).wait()
            row = pl.multiple_of(k * down_deep, down_deep)
            acc_c[...] += jnp.dot(
                hid[:, pl.ds(row, down_deep)] if downs_k > 1 else hid[...],
                down_ring[slot],
                preferred_element_type=jnp.float32,
            )
            start(i + slots)

        for i in range(chips):
            for part_ref, first in ((own_ref, 0), (lent_ref, chips * CAP)):
                part_ref[i, :, half * wide : (half + 1) * wide] = acc_c[
                    first + i * CAP : first + (i + 1) * CAP, :
                ].astype(jnp.bfloat16)


def ffn(mine, other, gate, held, up, down):
    chips, _, width = mine.shape
    rows = 2 * chips * CAP
    units = gate.shape[1]
    deep, wide = DEEP, width // 2
    slots = 11 if rows <= 64 else 6
    down_deep = min(deep, units)
    rings = [pltpu.VMEM((slots, deep, units), jnp.bfloat16)]
    if (down_deep, wide) != (deep, units):
        rings.append(pltpu.VMEM((slots, down_deep, wide), jnp.bfloat16))
    vmem = pl.BlockSpec(memory_space=pltpu.VMEM)
    return pl.pallas_call(
        functools.partial(ffn_kernel, deep, wide, [x.shape[0] // deep for x in held]),
        in_specs=[vmem] * 2 + [pl.BlockSpec(memory_space=pl.ANY)] * 3 + [vmem] * len(held),
        out_specs=[vmem, vmem],
        out_shape=[blocks_out(mine.shape)] * 2,
        scratch_shapes=[
            pltpu.SemaphoreType.DMA((slots,)),
            pltpu.VMEM((rows, width), jnp.bfloat16),
            pltpu.VMEM((rows, units), jnp.float32),
            pltpu.VMEM((rows, units), jnp.float32),
            pltpu.VMEM((rows, wide), jnp.float32),
            pltpu.VMEM((rows, units), jnp.bfloat16),
            *rings,
        ],
        compiler_params=pltpu.CompilerParams(vmem_limit_bytes=(34 if rows <= 64 else 52) * MIB),
        cost_estimate=pl.CostEstimate(
            flops=6 * rows * width * units,
            bytes_accessed=4 * width * units,
            transcendentals=rows * units,
        ),
        name="ffn",
    )(
        blocks_in_vmem(mine),
        blocks_in_vmem(other),
        in_hbm(gate),
        in_hbm(up),
        in_hbm(down),
        *[in_vmem(x) for x in held],
    )


def add_kernel(a_ref, b_ref, out_ref):
    chips = a_ref.shape[0]
    outers, inners = grid_of(chips)
    for i in range(chips):
        chip = partner_chips(chips, (i % inners) * outers + i // inners)
        out_ref[chip] = (a_ref[i].astype(jnp.float32) + b_ref[i].astype(jnp.float32)).astype(
            jnp.bfloat16
        )


def add(a, b):
    return pl.pallas_call(
        add_kernel,
        in_specs=[pl.BlockSpec(memory_space=pltpu.VMEM)] * 2,
        out_specs=pl.BlockSpec(memory_space=pltpu.VMEM),
        out_shape=blocks_out(a.shape),
        compiler_params=pltpu.CompilerParams(vmem_limit_bytes=16 * MIB),
        name="add",
    )(blocks_in_vmem(a), blocks_in_vmem(b))


def unpack_kernel(ids_ref, blocks_ref, out_ref, rows, out, sems):
    experts = lax.broadcasted_iota(jnp.int32, (rows.shape[0], 1), 0) // CAP
    layout = slot_layout(ids_ref[...], experts)
    copies = blocks_ref.shape[0] // EXP_FL
    for expert in range(EXP_FL):
        block = blocks_ref[expert * copies].astype(jnp.float32)
        for i in range(1, copies):
            block += blocks_ref[expert * copies + i].astype(jnp.float32)
        rows[expert * CAP : (expert + 1) * CAP, :] = block
    count = sems.shape[0]
    part = rows.shape[1] // count
    moves = []
    for i in range(count):
        columns = slice(i * part, (i + 1) * part)
        out[:, columns] = lax.dot_general(
            layout,
            rows[:, columns].astype(jnp.bfloat16),
            (((0,), (0,)), ((), ())),
            preferred_element_type=jnp.float32,
        ).astype(jnp.bfloat16)
        moves.append(pltpu.make_async_copy(out.at[:, columns], out_ref.at[:, columns], sems.at[i]))
        moves[-1].start()
    for move in moves:
        move.wait()


def unpack(blocks, ids):
    chips, _, width = blocks.shape
    shape = (ids.shape[1], width)
    return pl.pallas_call(
        unpack_kernel,
        in_specs=[pl.BlockSpec(memory_space=pltpu.VMEM)] * 2,
        out_specs=pl.BlockSpec(memory_space=pl.ANY),
        out_shape=jax.ShapeDtypeStruct(shape, jnp.bfloat16),
        scratch_shapes=[
            pltpu.VMEM((EXP_FL * CAP, width), jnp.float32),
            pltpu.VMEM(shape, jnp.bfloat16),
            pltpu.SemaphoreType.DMA((4,)),
        ],
        compiler_params=pltpu.CompilerParams(vmem_limit_bytes=16 * MIB),
        name="unpack",
    )(ids, blocks_in_vmem(blocks))


def per_device(tokens, expert_ids, norm_gain, router, gate_weight, up_weight, down_weight):
    devices = lax.axis_size("expert")
    chips = devices // 2
    outers, inners = grid_of(chips)
    same_core = [list(range(core, devices, 2)) for core in range(2)]
    ids = expert_ids.reshape(1, -1)

    def exchange(x, offset):
        return lax.ppermute(x, "expert", [(i, i ^ offset) for i in range(devices)])

    packed, held_a = pack(tokens, ids, norm_gain.reshape(1, -1), router.T, gate_weight, chips, 0, 2)
    arrived = [exchange(packed[i], 2 * i) for i in range(1, inners)]
    held_b = fetch(gate_weight, 2, 2)
    arrived, held_b = lax.optimization_barrier((arrived, held_b))
    near = [packed[0], *arrived]
    leaving = regroup(near, 1)
    far = [exchange(leaving[i - 1], 2 * inners * i) for i in range(1, outers)]
    leaving, gate = lax.optimization_barrier((leaving, gate_weight))
    held_c = fetch(gate, 4, 4)
    far, held_c = lax.optimization_barrier((far, held_c))
    mine = gather(near, far)
    other = exchange(mine, 1)
    own, lent = ffn(mine, other, gate_weight, (held_a, held_b, held_c), up_weight, down_weight)
    total = add(own, exchange(lent, 1))
    returned = lax.all_to_all(
        total, "expert", split_axis=0, concat_axis=0, tiled=True, axis_index_groups=same_core
    )
    return unpack(returned, ids)


def solution(mesh):
    in_specs = (
        P(("groups", "expert"), None),
        P(("groups", "expert")),
        P(),
        P(),
        P(None, "expert"),
        P(None, "expert"),
        P("expert", None),
    )
    out_specs = P(("groups", "expert"), None)
    return jax.shard_map(
        per_device, mesh=mesh, in_specs=in_specs, out_specs=out_specs, check_vma=False
    )
```

```python
import functools
import math

import jax
import jax.numpy as jnp
from jax import lax
from jax.experimental import pallas as pl
from jax.experimental.pallas import tpu as pltpu
from jax.sharding import PartitionSpec as P

EXP_FL = 8
CAP = 4
MIB = 1 << 20
DEEP = 512


def slot_layout(ids, experts):
    tokens = ids.shape[1]
    rows = experts.shape[0]
    expert = lax.broadcasted_iota(jnp.int32, (EXP_FL, tokens), 0)
    chosen = (jnp.broadcast_to(ids, (EXP_FL, tokens)) == expert).astype(jnp.float32)
    before = lax.broadcasted_iota(jnp.int32, (tokens, tokens), 0) < lax.broadcasted_iota(
        jnp.int32, (tokens, tokens), 1
    )
    earlier = jnp.dot(
        chosen.astype(jnp.bfloat16),
        before.astype(jnp.float32).astype(jnp.bfloat16),
        preferred_element_type=jnp.float32,
    )
    slot = jnp.sum(earlier * chosen, axis=0, keepdims=True).astype(jnp.int32)
    target = jnp.where(ids < EXP_FL, ids * CAP + slot, -1)
    row = experts * CAP + lax.broadcasted_iota(jnp.int32, (rows, 1), 0) % CAP
    return (row == jnp.broadcast_to(target, (rows, tokens))).astype(jnp.float32).astype(jnp.bfloat16)


def grid_of(chips):
    inner = 1 << (int(math.log2(chips)) // 2)
    return chips // inner, inner


def partner_chips(chips, index):
    outers, inners = grid_of(chips)
    here = lax.axis_index("expert") // 2
    return here ^ ((index % outers) * inners + index // outers)


def in_hbm(x):
    return pltpu.with_memory_space_constraint(x, pltpu.HBM)


def in_vmem(x):
    return pltpu.with_memory_space_constraint(x, pltpu.VMEM)


def blocks_in_vmem(x):
    return in_vmem(x) if x.size <= MIB else x


def blocks_out(shape):
    if math.prod(shape) <= MIB:
        return pltpu.VMEM(shape, jnp.bfloat16)
    return jax.ShapeDtypeStruct(shape, jnp.bfloat16)


def join_rows(blocks_ref, rows_ref, first):
    for i in range(blocks_ref.shape[0]):
        rows_ref[first + i * CAP : first + (i + 1) * CAP, :] = blocks_ref[i].astype(rows_ref.dtype)


def pack_kernel(outers, *refs):
    ids_ref, tokens_ref, gain_ref, router_ref = refs[:4]
    outs, (ids, tokens, gain, router, sems) = refs[5:-5], refs[-5:]
    pairs = ((ids_ref, ids), (tokens_ref, tokens), (gain_ref, gain), (router_ref, router))
    moves = [pltpu.make_async_copy(a, b, sems.at[i]) for i, (a, b) in enumerate(pairs)]
    for move in moves:
        move.start()
    inners = len(outs)
    chips = outers * inners
    rows = chips * CAP
    copies = chips // EXP_FL
    index = lax.broadcasted_iota(jnp.int32, (rows, 1), 0) // CAP
    experts = partner_chips(chips, index) // copies
    moves[0].wait()
    layout = slot_layout(ids[...], experts)
    moves[1].wait()
    packed = jnp.dot(layout, tokens[...], preferred_element_type=jnp.float32)
    mean_square = jnp.mean(packed * packed, axis=-1, keepdims=True)
    moves[2].wait()
    normed = (packed * lax.rsqrt(mean_square + 1e-05) * gain[...]).astype(jnp.bfloat16)
    moves[3].wait()
    logits = lax.dot_general(
        normed, router[...], (((1,), (1,)), ((), ())), preferred_element_type=jnp.float32
    )
    own = lax.broadcasted_iota(jnp.int32, logits.shape, 1) == experts
    logit = jnp.sum(jnp.where(own, logits, 0.0), axis=-1, keepdims=True)
    routed = normed.astype(jnp.float32) * jax.nn.sigmoid(logit)
    for i in range(chips):
        outs[i // outers][i % outers] = routed[i * CAP : (i + 1) * CAP].astype(jnp.bfloat16)


def pack(tokens, ids, gain, router_rows, weight, chips):
    width = tokens.shape[1]
    outers, inners = grid_of(chips)
    arrays = (ids, tokens, gain, router_rows)
    return pl.pallas_call(
        functools.partial(pack_kernel, outers),
        in_specs=[pl.BlockSpec(memory_space=pl.ANY)] * 5,
        out_specs=[pl.BlockSpec(memory_space=pltpu.VMEM)] * inners,
        out_shape=[blocks_out((outers, CAP, width))] * inners,
        scratch_shapes=[pltpu.VMEM(x.shape, x.dtype) for x in arrays]
        + [pltpu.SemaphoreType.DMA((4,))],
        compiler_params=pltpu.CompilerParams(vmem_limit_bytes=(12 if chips <= 8 else 40) * MIB),
        name="pack",
    )(*[in_hbm(x) for x in (*arrays, weight)])


def regroup_kernel(first, groups, *refs):
    for i, out_ref in enumerate(refs[groups:]):
        for j in range(groups):
            out_ref[j] = refs[j][first + i]


def regroup(arrays, first):
    count, _, width = arrays[0].shape
    vmem = pl.BlockSpec(memory_space=pltpu.VMEM)
    return pl.pallas_call(
        functools.partial(regroup_kernel, first, len(arrays)),
        in_specs=[vmem] * len(arrays),
        out_specs=[vmem] * (count - first),
        out_shape=[blocks_out((len(arrays), CAP, width))] * (count - first),
        compiler_params=pltpu.CompilerParams(vmem_limit_bytes=(4 if count <= 8 else 24) * MIB),
        name="regroup",
    )(*[blocks_in_vmem(x) for x in arrays])


def gather_kernel(kept, *refs):
    out_ref = refs[-1]
    for i in range(kept):
        out_ref[i] = refs[i][0]
    for i, ref in enumerate(refs[kept:-1]):
        out_ref[(i + 1) * kept : (i + 2) * kept] = ref[...]


def gather(kept, arrived):
    arrays = (*kept, *arrived)
    _, _, width = kept[0].shape
    chips = len(kept) * (len(arrived) + 1)
    return pl.pallas_call(
        functools.partial(gather_kernel, len(kept)),
        in_specs=[pl.BlockSpec(memory_space=pltpu.VMEM)] * len(arrays),
        out_specs=pl.BlockSpec(memory_space=pltpu.VMEM),
        out_shape=blocks_out((chips, CAP, width)),
        compiler_params=pltpu.CompilerParams(vmem_limit_bytes=(4 if chips <= 8 else 24) * MIB),
        name="gather",
    )(*[blocks_in_vmem(x) for x in arrays])


def ffn_kernel(
    deep,
    wide,
    mine_ref,
    other_ref,
    up_ref,
    down_ref,
    gate_ref,
    own_ref,
    lent_ref,
    sems,
    x_ref,
    acc_a,
    acc_b,
    acc_c,
    hid,
    ring,
    *rings,
):
    down_ring = rings[0] if rings else ring
    chips, _, width = mine_ref.shape
    units = gate_ref.shape[1]
    slots = ring.shape[0]
    ups = width // deep
    down_deep = min(deep, units)
    downs_k = units // down_deep
    halves = width // wide
    total = ups + halves * downs_k

    def up_copy(i):
        slot = lax.rem(i, slots)
        row = pl.multiple_of(i * deep, deep)
        return pltpu.make_async_copy(up_ref.at[pl.ds(row, deep)], ring.at[slot], sems.at[slot])

    def down_copy(i):
        slot = lax.rem(i, slots)
        j = i - ups
        row = pl.multiple_of(lax.rem(j, downs_k) * down_deep, down_deep)
        col = pl.multiple_of((j // downs_k) * wide, wide)
        return pltpu.make_async_copy(
            down_ref.at[pl.ds(row, down_deep), pl.ds(col, wide)],
            down_ring.at[slot],
            sems.at[slot],
        )

    def start(i):
        @pl.when(i < ups)
        def _():
            up_copy(i).start()

        @pl.when(jnp.logical_and(i >= ups, i < total))
        def _():
            down_copy(i).start()

    @pl.loop(0, min(slots, total))
    def _(i):
        start(i)

    join_rows(mine_ref, x_ref, 0)
    join_rows(other_ref, x_ref, chips * CAP)
    acc_a[...] = jnp.zeros_like(acc_a)
    acc_b[...] = jnp.zeros_like(acc_b)

    @pl.loop(0, ups)
    def _(i):
        row = pl.multiple_of(i * deep, deep)
        acc_a[...] += jnp.dot(
            x_ref[:, pl.ds(row, deep)],
            gate_ref[pl.ds(row, deep), :],
            preferred_element_type=jnp.float32,
        )

    @pl.loop(0, ups)
    def _(i):
        row = pl.multiple_of(i * deep, deep)
        up_copy(i).wait()
        acc_b[...] += jnp.dot(
            x_ref[:, pl.ds(row, deep)], ring[lax.rem(i, slots)], preferred_element_type=jnp.float32
        )
        start(i + slots)

    gate = acc_a[...]
    hid[...] = (gate / (1.0 + jnp.exp(-gate)) * acc_b[...]).astype(jnp.bfloat16)

    for half in range(halves):
        acc_c[...] = jnp.zeros_like(acc_c)

        @pl.loop(0, downs_k)
        def _(k, half=half):
            i = ups + half * downs_k + k
            slot = lax.rem(i, slots)
            down_copy(i).wait()
            row = pl.multiple_of(k * down_deep, down_deep)
            acc_c[...] += jnp.dot(
                hid[:, pl.ds(row, down_deep)] if downs_k > 1 else hid[...],
                down_ring[slot],
                preferred_element_type=jnp.float32,
            )
            start(i + slots)

        for i in range(chips):
            for part_ref, first in ((own_ref, 0), (lent_ref, chips * CAP)):
                part_ref[i, :, half * wide : (half + 1) * wide] = acc_c[
                    first + i * CAP : first + (i + 1) * CAP, :
                ].astype(jnp.bfloat16)


def ffn(mine, other, gate, up, down):
    chips, _, width = mine.shape
    rows = 2 * chips * CAP
    units = gate.shape[1]
    deep, wide = DEEP, width // 2
    slots = 11 if rows <= 64 else 6
    down_deep = min(deep, units)
    rings = [pltpu.VMEM((slots, deep, units), jnp.bfloat16)]
    if (down_deep, wide) != (deep, units):
        rings.append(pltpu.VMEM((slots, down_deep, wide), jnp.bfloat16))
    vmem = pl.BlockSpec(memory_space=pltpu.VMEM)
    return pl.pallas_call(
        functools.partial(ffn_kernel, deep, wide),
        in_specs=[vmem] * 2 + [pl.BlockSpec(memory_space=pl.ANY)] * 2 + [vmem],
        out_specs=[vmem, vmem],
        out_shape=[blocks_out(mine.shape)] * 2,
        scratch_shapes=[
            pltpu.SemaphoreType.DMA((slots,)),
            pltpu.VMEM((rows, width), jnp.bfloat16),
            pltpu.VMEM((rows, units), jnp.float32),
            pltpu.VMEM((rows, units), jnp.float32),
            pltpu.VMEM((rows, wide), jnp.float32),
            pltpu.VMEM((rows, units), jnp.bfloat16),
            *rings,
        ],
        compiler_params=pltpu.CompilerParams(vmem_limit_bytes=(34 if rows <= 64 else 52) * MIB),
        cost_estimate=pl.CostEstimate(
            flops=6 * rows * width * units,
            bytes_accessed=4 * width * units,
            transcendentals=rows * units,
        ),
        name="ffn",
    )(
        blocks_in_vmem(mine),
        blocks_in_vmem(other),
        in_hbm(up),
        in_hbm(down),
        in_vmem(gate),
    )


def add_kernel(a_ref, b_ref, out_ref):
    chips = a_ref.shape[0]
    outers, inners = grid_of(chips)
    for i in range(chips):
        chip = partner_chips(chips, (i % inners) * outers + i // inners)
        out_ref[chip] = (a_ref[i].astype(jnp.float32) + b_ref[i].astype(jnp.float32)).astype(
            jnp.bfloat16
        )


def add(a, b):
    return pl.pallas_call(
        add_kernel,
        in_specs=[pl.BlockSpec(memory_space=pltpu.VMEM)] * 2,
        out_specs=pl.BlockSpec(memory_space=pltpu.VMEM),
        out_shape=blocks_out(a.shape),
        compiler_params=pltpu.CompilerParams(vmem_limit_bytes=16 * MIB),
        name="add",
    )(blocks_in_vmem(a), blocks_in_vmem(b))


def unpack_kernel(ids_ref, blocks_ref, out_ref, rows, out, sems):
    experts = lax.broadcasted_iota(jnp.int32, (rows.shape[0], 1), 0) // CAP
    layout = slot_layout(ids_ref[...], experts)
    copies = blocks_ref.shape[0] // EXP_FL
    for expert in range(EXP_FL):
        block = blocks_ref[expert * copies].astype(jnp.float32)
        for i in range(1, copies):
            block += blocks_ref[expert * copies + i].astype(jnp.float32)
        rows[expert * CAP : (expert + 1) * CAP, :] = block
    count = sems.shape[0]
    part = rows.shape[1] // count
    moves = []
    for i in range(count):
        columns = slice(i * part, (i + 1) * part)
        out[:, columns] = lax.dot_general(
            layout,
            rows[:, columns].astype(jnp.bfloat16),
            (((0,), (0,)), ((), ())),
            preferred_element_type=jnp.float32,
        ).astype(jnp.bfloat16)
        moves.append(pltpu.make_async_copy(out.at[:, columns], out_ref.at[:, columns], sems.at[i]))
        moves[-1].start()
    for move in moves:
        move.wait()


def unpack(blocks, ids):
    chips, _, width = blocks.shape
    shape = (ids.shape[1], width)
    return pl.pallas_call(
        unpack_kernel,
        in_specs=[pl.BlockSpec(memory_space=pltpu.VMEM)] * 2,
        out_specs=pl.BlockSpec(memory_space=pl.ANY),
        out_shape=jax.ShapeDtypeStruct(shape, jnp.bfloat16),
        scratch_shapes=[
            pltpu.VMEM((EXP_FL * CAP, width), jnp.float32),
            pltpu.VMEM(shape, jnp.bfloat16),
            pltpu.SemaphoreType.DMA((4,)),
        ],
        compiler_params=pltpu.CompilerParams(vmem_limit_bytes=16 * MIB),
        name="unpack",
    )(ids, blocks_in_vmem(blocks))


def per_device(tokens, expert_ids, norm_gain, router, gate_weight, up_weight, down_weight):
    devices = lax.axis_size("expert")
    chips = devices // 2
    outers, inners = grid_of(chips)
    same_core = [list(range(core, devices, 2)) for core in range(2)]
    ids = expert_ids.reshape(1, -1)

    def exchange(x, offset):
        return lax.ppermute(x, "expert", [(i, i ^ offset) for i in range(devices)])

    packed = pack(tokens, ids, norm_gain.reshape(1, -1), router.T, up_weight, chips)
    near = [packed[0], *[exchange(packed[i], 2 * i) for i in range(1, inners)]]
    leaving = regroup(near, 1)
    far = [exchange(leaving[i - 1], 2 * inners * i) for i in range(1, outers)]
    mine = gather(near, far)
    own, lent = ffn(mine, exchange(mine, 1), gate_weight, up_weight, down_weight)
    total = add(own, exchange(lent, 1))
    returned = lax.all_to_all(
        total, "expert", split_axis=0, concat_axis=0, tiled=True, axis_index_groups=same_core
    )
    return unpack(returned, ids)


def solution(mesh):
    in_specs = (
        P(("groups", "expert"), None),
        P(("groups", "expert")),
        P(),
        P(),
        P(None, "expert"),
        P(None, "expert"),
        P("expert", None),
    )
    out_specs = P(("groups", "expert"), None)
    return jax.shard_map(
        per_device, mesh=mesh, in_specs=in_specs, out_specs=out_specs, check_vma=False
    )
```

```python
import functools
import math

import jax
import jax.numpy as jnp
from jax import lax
from jax.experimental import pallas as pl
from jax.experimental.pallas import tpu as pltpu
from jax.sharding import PartitionSpec as P

EXP_FL = 8
CAP = 4
MIB = 1 << 20
DEEP = 512


def token_rows(ids):
    tokens = ids.shape[1]
    expert = lax.broadcasted_iota(jnp.int32, (EXP_FL, tokens), 0)
    chosen = (jnp.broadcast_to(ids, (EXP_FL, tokens)) == expert).astype(jnp.float32)
    before = lax.broadcasted_iota(jnp.int32, (tokens, tokens), 0) < lax.broadcasted_iota(
        jnp.int32, (tokens, tokens), 1
    )
    earlier = jnp.dot(
        chosen.astype(jnp.bfloat16),
        before.astype(jnp.float32).astype(jnp.bfloat16),
        preferred_element_type=jnp.float32,
    )
    slot = jnp.sum(earlier * chosen, axis=0, keepdims=True).astype(jnp.int32)
    return jnp.where(ids < EXP_FL, ids * CAP + slot, -1)


def slot_layout(target, experts):
    rows, tokens = experts.shape[0], target.shape[1]
    row = experts * CAP + lax.broadcasted_iota(jnp.int32, (rows, 1), 0) % CAP
    return (row == jnp.broadcast_to(target, (rows, tokens))).astype(jnp.float32).astype(jnp.bfloat16)


def grid_of(chips):
    inner = 1 << (int(math.log2(chips)) // 2)
    return chips // inner, inner


def partner_chips(chips, index):
    outers, inners = grid_of(chips)
    here = lax.axis_index("expert") // 2
    return here ^ (index % outers * inners + index // outers)


def in_hbm(x):
    return pltpu.with_memory_space_constraint(x, pltpu.HBM)


def in_vmem(x):
    return pltpu.with_memory_space_constraint(x, pltpu.VMEM)


def blocks_in_vmem(x):
    return in_vmem(x) if x.size <= MIB else x


def blocks_out(shape):
    if math.prod(shape) <= MIB:
        return pltpu.VMEM(shape, jnp.bfloat16)
    return jax.ShapeDtypeStruct(shape, jnp.bfloat16)


def join_rows(blocks_ref, rows_ref, first):
    for i in range(blocks_ref.shape[0]):
        rows_ref[first + i * CAP : first + (i + 1) * CAP, :] = blocks_ref[i].astype(rows_ref.dtype)


def store_blocks(values, singles, groups):
    outers = len(singles)
    for i in range(values.shape[0] // CAP):
        block = values[i * CAP : (i + 1) * CAP].astype(jnp.bfloat16)
        if i < outers:
            singles[i][0] = block
        else:
            groups[i // outers - 1][i % outers] = block


def blocks_shapes(chips, width):
    outers, inners = grid_of(chips)
    return [blocks_out((1, CAP, width))] * outers + [blocks_out((outers, CAP, width))] * (inners - 1)


def pack_kernel(outers, *refs):
    ids_ref, tokens_ref, gain_ref, router_ref = refs[:4]
    outs, target_ref = refs[5:-6], refs[-6]
    ids, tokens, gain, router, sems = refs[-5:]
    pairs = ((ids_ref, ids), (tokens_ref, tokens), (gain_ref, gain), (router_ref, router))
    moves = [pltpu.make_async_copy(a, b, sems.at[i]) for i, (a, b) in enumerate(pairs)]
    for move in moves:
        move.start()
    inners = len(outs) - outers + 1
    chips = outers * inners
    rows = chips * CAP
    copies = chips // EXP_FL
    index = lax.broadcasted_iota(jnp.int32, (rows, 1), 0) // CAP
    experts = partner_chips(chips, index) // copies
    moves[0].wait()
    target = token_rows(ids[...])
    target_ref[...] = target
    layout = slot_layout(target, experts)
    moves[1].wait()
    packed = jnp.dot(layout, tokens[...], preferred_element_type=jnp.float32)
    mean_square = jnp.mean(packed * packed, axis=-1, keepdims=True)
    moves[2].wait()
    normed = (packed * lax.rsqrt(mean_square + 1e-05) * gain[...]).astype(jnp.bfloat16)
    moves[3].wait()
    logits = lax.dot_general(
        normed, router[...], (((1,), (1,)), ((), ())), preferred_element_type=jnp.float32
    )
    own = lax.broadcasted_iota(jnp.int32, logits.shape, 1) == experts
    logit = jnp.sum(jnp.where(own, logits, 0.0), axis=-1, keepdims=True)
    routed = normed.astype(jnp.float32) * jax.nn.sigmoid(logit)
    store_blocks(routed, outs[:outers], outs[outers:])


def pack(tokens, ids, gain, router_rows, weight, chips):
    width = tokens.shape[1]
    outers, inners = grid_of(chips)
    arrays = (ids, tokens, gain, router_rows)
    outs = pl.pallas_call(
        functools.partial(pack_kernel, outers),
        in_specs=[pl.BlockSpec(memory_space=pl.ANY)] * 5,
        out_specs=[pl.BlockSpec(memory_space=pltpu.VMEM)] * (outers + inners),
        out_shape=blocks_shapes(chips, width) + [pltpu.VMEM(ids.shape, jnp.int32)],
        scratch_shapes=[pltpu.VMEM(x.shape, x.dtype) for x in arrays]
        + [pltpu.SemaphoreType.DMA((4,))],
        compiler_params=pltpu.CompilerParams(vmem_limit_bytes=(12 if chips <= 8 else 40) * MIB),
        name="pack",
    )(*[in_hbm(x) for x in (*arrays, weight)])
    return outs[:-1], outs[-1]


def forward_kernel(groups, *refs):
    for i, out_ref in enumerate(refs[groups:]):
        for j in range(groups):
            out_ref[j] = refs[j][i + 1]


def forward(arrays):
    outers, _, width = arrays[0].shape
    vmem = pl.BlockSpec(memory_space=pltpu.VMEM)
    return pl.pallas_call(
        functools.partial(forward_kernel, len(arrays)),
        in_specs=[vmem] * len(arrays),
        out_specs=[vmem] * (outers - 1),
        out_shape=[blocks_out((len(arrays), CAP, width))] * (outers - 1),
        compiler_params=pltpu.CompilerParams(vmem_limit_bytes=(4 if outers <= 4 else 24) * MIB),
        name="forward",
    )(*[blocks_in_vmem(x) for x in arrays])


def piece_blocks(outers, inners, refs):
    singles, groups, forwarded = refs[:outers], refs[outers : outers + inners - 1], refs[outers + inners - 1 :]
    for i in range(outers):
        yield i, singles[i][0]
    for i in range(1, inners):
        yield i * outers, groups[i - 1][0]
        for j in range(1, outers):
            yield i * outers + j, forwarded[j - 1][i - 1]


def gather_kernel(outers, inners, *refs):
    for i, block in piece_blocks(outers, inners, refs[:-1]):
        refs[-1][i] = block


def gather(pieces, chips):
    outers, inners = grid_of(chips)
    width = pieces[0].shape[2]
    vmem = pl.BlockSpec(memory_space=pltpu.VMEM)
    return pl.pallas_call(
        functools.partial(gather_kernel, outers, inners),
        in_specs=[vmem] * len(pieces),
        out_specs=vmem,
        out_shape=blocks_out((chips, CAP, width)),
        compiler_params=pltpu.CompilerParams(vmem_limit_bytes=(4 if chips <= 8 else 24) * MIB),
        name="gather",
    )(*[blocks_in_vmem(x) for x in pieces])


def ffn_kernel(
    deep,
    wide,
    mine_ref,
    other_ref,
    up_ref,
    down_ref,
    gate_ref,
    own_ref,
    lent_ref,
    sems,
    x_ref,
    acc_a,
    acc_b,
    acc_c,
    hid,
    ring,
    *rings,
):
    down_ring = rings[0] if rings else ring
    chips, _, width = mine_ref.shape
    units = gate_ref.shape[1]
    slots = ring.shape[0]
    ups = width // deep
    down_deep = min(deep, units)
    downs_k = units // down_deep
    halves = width // wide
    total = ups + halves * downs_k

    def up_copy(i):
        slot = lax.rem(i, slots)
        row = pl.multiple_of(i * deep, deep)
        return pltpu.make_async_copy(up_ref.at[pl.ds(row, deep)], ring.at[slot], sems.at[slot])

    def down_copy(i):
        slot = lax.rem(i, slots)
        j = i - ups
        row = pl.multiple_of(lax.rem(j, downs_k) * down_deep, down_deep)
        col = pl.multiple_of((j // downs_k) * wide, wide)
        return pltpu.make_async_copy(
            down_ref.at[pl.ds(row, down_deep), pl.ds(col, wide)],
            down_ring.at[slot],
            sems.at[slot],
        )

    def start(i):
        @pl.when(i < ups)
        def _():
            up_copy(i).start()

        @pl.when(jnp.logical_and(i >= ups, i < total))
        def _():
            down_copy(i).start()

    @pl.loop(0, min(slots, total))
    def _(i):
        start(i)

    join_rows(mine_ref, x_ref, 0)
    join_rows(other_ref, x_ref, chips * CAP)
    acc_a[...] = jnp.zeros_like(acc_a)
    acc_b[...] = jnp.zeros_like(acc_b)

    @pl.loop(0, ups)
    def _(i):
        row = pl.multiple_of(i * deep, deep)
        acc_a[...] += jnp.dot(
            x_ref[:, pl.ds(row, deep)],
            gate_ref[pl.ds(row, deep), :],
            preferred_element_type=jnp.float32,
        )

    @pl.loop(0, ups)
    def _(i):
        row = pl.multiple_of(i * deep, deep)
        up_copy(i).wait()
        acc_b[...] += jnp.dot(
            x_ref[:, pl.ds(row, deep)], ring[lax.rem(i, slots)], preferred_element_type=jnp.float32
        )
        start(i + slots)

    gate = acc_a[...]
    hid[...] = (gate / (1.0 + jnp.exp(-gate)) * acc_b[...]).astype(jnp.bfloat16)

    for half in range(halves):
        acc_c[...] = jnp.zeros_like(acc_c)

        @pl.loop(0, downs_k)
        def _(k, half=half):
            i = ups + half * downs_k + k
            slot = lax.rem(i, slots)
            down_copy(i).wait()
            row = pl.multiple_of(k * down_deep, down_deep)
            acc_c[...] += jnp.dot(
                hid[:, pl.ds(row, down_deep)] if downs_k > 1 else hid[...],
                down_ring[slot],
                preferred_element_type=jnp.float32,
            )
            start(i + slots)

        for i in range(chips):
            for part_ref, first in ((own_ref, 0), (lent_ref, chips * CAP)):
                part_ref[i, :, half * wide : (half + 1) * wide] = acc_c[
                    first + i * CAP : first + (i + 1) * CAP, :
                ].astype(jnp.bfloat16)


def ffn(mine, other, gate, up, down):
    chips, _, width = mine.shape
    rows = 2 * chips * CAP
    units = gate.shape[1]
    deep, wide = DEEP, width // 2
    slots = 11 if rows <= 64 else 6
    down_deep = min(deep, units)
    rings = [pltpu.VMEM((slots, deep, units), jnp.bfloat16)]
    if (down_deep, wide) != (deep, units):
        rings.append(pltpu.VMEM((slots, down_deep, wide), jnp.bfloat16))
    vmem = pl.BlockSpec(memory_space=pltpu.VMEM)
    return pl.pallas_call(
        functools.partial(ffn_kernel, deep, wide),
        in_specs=[vmem] * 2 + [pl.BlockSpec(memory_space=pl.ANY)] * 2 + [vmem],
        out_specs=[vmem, vmem],
        out_shape=[blocks_out(mine.shape)] * 2,
        scratch_shapes=[
            pltpu.SemaphoreType.DMA((slots,)),
            pltpu.VMEM((rows, width), jnp.bfloat16),
            pltpu.VMEM((rows, units), jnp.float32),
            pltpu.VMEM((rows, units), jnp.float32),
            pltpu.VMEM((rows, wide), jnp.float32),
            pltpu.VMEM((rows, units), jnp.bfloat16),
            *rings,
        ],
        compiler_params=pltpu.CompilerParams(vmem_limit_bytes=(34 if rows <= 64 else 52) * MIB),
        cost_estimate=pl.CostEstimate(
            flops=6 * rows * width * units,
            bytes_accessed=4 * width * units,
            transcendentals=rows * units,
        ),
        name="ffn",
    )(
        blocks_in_vmem(mine),
        blocks_in_vmem(other),
        in_hbm(up),
        in_hbm(down),
        in_vmem(gate),
    )


def add_kernel(a_ref, b_ref, out_ref):
    chips = a_ref.shape[0]
    for i in range(chips):
        chip = partner_chips(chips, i)
        out_ref[chip] = (a_ref[i].astype(jnp.float32) + b_ref[i].astype(jnp.float32)).astype(
            jnp.bfloat16
        )


def add(a, b):
    return pl.pallas_call(
        add_kernel,
        in_specs=[pl.BlockSpec(memory_space=pltpu.VMEM)] * 2,
        out_specs=pl.BlockSpec(memory_space=pltpu.VMEM),
        out_shape=blocks_out(a.shape),
        compiler_params=pltpu.CompilerParams(vmem_limit_bytes=16 * MIB),
        name="add",
    )(blocks_in_vmem(a), blocks_in_vmem(b))


def unpack_kernel(target_ref, blocks_ref, out_ref, rows, out, sems):
    experts = lax.broadcasted_iota(jnp.int32, (rows.shape[0], 1), 0) // CAP
    layout = slot_layout(target_ref[...], experts)
    copies = blocks_ref.shape[0] // EXP_FL
    for expert in range(EXP_FL):
        block = blocks_ref[expert * copies].astype(jnp.float32)
        for i in range(1, copies):
            block += blocks_ref[expert * copies + i].astype(jnp.float32)
        rows[expert * CAP : (expert + 1) * CAP, :] = block
    count = sems.shape[0]
    part = rows.shape[1] // count
    moves = []
    for i in range(count):
        columns = slice(i * part, (i + 1) * part)
        out[:, columns] = lax.dot_general(
            layout,
            rows[:, columns].astype(jnp.bfloat16),
            (((0,), (0,)), ((), ())),
            preferred_element_type=jnp.float32,
        ).astype(jnp.bfloat16)
        moves.append(pltpu.make_async_copy(out.at[:, columns], out_ref.at[:, columns], sems.at[i]))
        moves[-1].start()
    for move in moves:
        move.wait()


def unpack(blocks, target):
    chips, _, width = blocks.shape
    shape = (target.shape[1], width)
    return pl.pallas_call(
        unpack_kernel,
        in_specs=[pl.BlockSpec(memory_space=pltpu.VMEM)] * 2,
        out_specs=pl.BlockSpec(memory_space=pl.ANY),
        out_shape=jax.ShapeDtypeStruct(shape, jnp.bfloat16),
        scratch_shapes=[
            pltpu.VMEM((EXP_FL * CAP, width), jnp.float32),
            pltpu.VMEM(shape, jnp.bfloat16),
            pltpu.SemaphoreType.DMA((4,)),
        ],
        compiler_params=pltpu.CompilerParams(vmem_limit_bytes=16 * MIB),
        name="unpack",
    )(in_vmem(target), blocks_in_vmem(blocks))


def per_device(tokens, expert_ids, norm_gain, router, gate_weight, up_weight, down_weight):
    devices = lax.axis_size("expert")
    chips = devices // 2
    outers, inners = grid_of(chips)
    same_core = [list(range(core, devices, 2)) for core in range(2)]
    ids = expert_ids.reshape(1, -1)

    def exchange(x, offset):
        return lax.ppermute(x, "expert", [(i, i ^ offset) for i in range(devices)])

    blocks, target = pack(tokens, ids, norm_gain.reshape(1, -1), router.T, up_weight, chips)
    singles, groups = blocks[:outers], blocks[outers:]
    steps = [2 * inners * i for i in range(1, outers)]
    near = [exchange(x, 2 * (i + 1)) for i, x in enumerate(groups)]
    direct = [exchange(x, step) for x, step in zip(singles[1:], steps)]
    onward = [exchange(x, step) for x, step in zip(forward(near), steps)]
    mine = gather([singles[0], *direct, *near, *onward], chips)
    own, lent = ffn(mine, exchange(mine, 1), gate_weight, up_weight, down_weight)
    total = add(own, exchange(lent, 1))
    returned = lax.all_to_all(
        total, "expert", split_axis=0, concat_axis=0, tiled=True, axis_index_groups=same_core
    )
    return unpack(returned, target)


def solution(mesh):
    in_specs = (
        P(("groups", "expert"), None),
        P(("groups", "expert")),
        P(),
        P(),
        P(None, "expert"),
        P(None, "expert"),
        P("expert", None),
    )
    out_specs = P(("groups", "expert"), None)
    return jax.shard_map(
        per_device, mesh=mesh, in_specs=in_specs, out_specs=out_specs, check_vma=False
    )
```

```python
import functools
import math

import jax
import jax.numpy as jnp
from jax import lax
from jax.experimental import pallas as pl
from jax.experimental.pallas import tpu as pltpu
from jax.sharding import PartitionSpec as P

EXP_FL = 8
CAP = 4
MIB = 1 << 20
DEEP = 512


def token_rows(ids):
    tokens = ids.shape[1]
    expert = lax.broadcasted_iota(jnp.int32, (EXP_FL, tokens), 0)
    chosen = (jnp.broadcast_to(ids, (EXP_FL, tokens)) == expert).astype(jnp.float32)
    before = lax.broadcasted_iota(jnp.int32, (tokens, tokens), 0) < lax.broadcasted_iota(
        jnp.int32, (tokens, tokens), 1
    )
    earlier = jnp.dot(
        chosen.astype(jnp.bfloat16),
        before.astype(jnp.float32).astype(jnp.bfloat16),
        preferred_element_type=jnp.float32,
    )
    slot = jnp.sum(earlier * chosen, axis=0, keepdims=True).astype(jnp.int32)
    return jnp.where(ids < EXP_FL, ids * CAP + slot, -1)


def slot_layout(target, experts):
    rows, tokens = experts.shape[0], target.shape[1]
    row = experts * CAP + lax.broadcasted_iota(jnp.int32, (rows, 1), 0) % CAP
    return (row == jnp.broadcast_to(target, (rows, tokens))).astype(jnp.float32).astype(jnp.bfloat16)


def grid_of(chips):
    inner = 1 << (int(math.log2(chips)) // 2)
    return chips // inner, inner


def partner_chips(chips, index):
    outers, inners = grid_of(chips)
    here = lax.axis_index("expert") // 2
    return here ^ (index % outers * inners + index // outers)


def in_hbm(x):
    return pltpu.with_memory_space_constraint(x, pltpu.HBM)


def in_vmem(x):
    return pltpu.with_memory_space_constraint(x, pltpu.VMEM)


def blocks_in_vmem(x):
    return in_vmem(x) if x.size <= MIB else x


def blocks_out(shape):
    if math.prod(shape) <= MIB:
        return pltpu.VMEM(shape, jnp.bfloat16)
    return jax.ShapeDtypeStruct(shape, jnp.bfloat16)


def join_rows(blocks_ref, rows_ref, first):
    for i in range(blocks_ref.shape[0]):
        rows_ref[first + i * CAP : first + (i + 1) * CAP, :] = blocks_ref[i].astype(rows_ref.dtype)


def store_blocks(values, singles, groups):
    outers = len(singles)
    for i in range(values.shape[0] // CAP):
        block = values[i * CAP : (i + 1) * CAP].astype(jnp.bfloat16)
        if i < outers:
            singles[i][0] = block
        else:
            groups[i // outers - 1][i % outers] = block


def blocks_shapes(chips, width):
    outers, inners = grid_of(chips)
    return [blocks_out((1, CAP, width))] * outers + [blocks_out((outers, CAP, width))] * (inners - 1)


def pack_kernel(outers, *refs):
    ids_ref, tokens_ref, gain_ref, router_ref = refs[:4]
    outs, target_ref = refs[5:-6], refs[-6]
    ids, tokens, gain, router, sems = refs[-5:]
    pairs = ((ids_ref, ids), (tokens_ref, tokens), (gain_ref, gain), (router_ref, router))
    moves = [pltpu.make_async_copy(a, b, sems.at[i]) for i, (a, b) in enumerate(pairs)]
    for move in moves:
        move.start()
    inners = len(outs) - outers + 1
    chips = outers * inners
    rows = chips * CAP
    copies = chips // EXP_FL
    index = lax.broadcasted_iota(jnp.int32, (rows, 1), 0) // CAP
    experts = partner_chips(chips, index) // copies
    moves[0].wait()
    target = token_rows(ids[...])
    target_ref[...] = target
    layout = slot_layout(target, experts)
    moves[1].wait()
    packed = jnp.dot(layout, tokens[...], preferred_element_type=jnp.float32)
    mean_square = jnp.mean(packed * packed, axis=-1, keepdims=True)
    moves[2].wait()
    normed = (packed * lax.rsqrt(mean_square + 1e-05) * gain[...]).astype(jnp.bfloat16)
    moves[3].wait()
    logits = lax.dot_general(
        normed, router[...], (((1,), (1,)), ((), ())), preferred_element_type=jnp.float32
    )
    own = lax.broadcasted_iota(jnp.int32, logits.shape, 1) == experts
    logit = jnp.sum(jnp.where(own, logits, 0.0), axis=-1, keepdims=True)
    routed = normed.astype(jnp.float32) * jax.nn.sigmoid(logit)
    store_blocks(routed, outs[:outers], outs[outers:])


def pack(tokens, ids, gain, router_rows, weight, chips):
    width = tokens.shape[1]
    outers, inners = grid_of(chips)
    arrays = (ids, tokens, gain, router_rows)
    outs = pl.pallas_call(
        functools.partial(pack_kernel, outers),
        in_specs=[pl.BlockSpec(memory_space=pl.ANY)] * 5,
        out_specs=[pl.BlockSpec(memory_space=pltpu.VMEM)] * (outers + inners),
        out_shape=blocks_shapes(chips, width) + [pltpu.VMEM(ids.shape, jnp.int32)],
        scratch_shapes=[pltpu.VMEM(x.shape, x.dtype) for x in arrays]
        + [pltpu.SemaphoreType.DMA((4,))],
        compiler_params=pltpu.CompilerParams(vmem_limit_bytes=(12 if chips <= 8 else 40) * MIB),
        name="pack",
    )(*[in_hbm(x) for x in (*arrays, weight)])
    return outs[:-1], outs[-1]


def forward_kernel(groups, *refs):
    for i, out_ref in enumerate(refs[groups:]):
        for j in range(groups):
            out_ref[j] = refs[j][i + 1]


def forward(arrays):
    outers, _, width = arrays[0].shape
    vmem = pl.BlockSpec(memory_space=pltpu.VMEM)
    return pl.pallas_call(
        functools.partial(forward_kernel, len(arrays)),
        in_specs=[vmem] * len(arrays),
        out_specs=[vmem] * (outers - 1),
        out_shape=[blocks_out((len(arrays), CAP, width))] * (outers - 1),
        compiler_params=pltpu.CompilerParams(vmem_limit_bytes=(4 if outers <= 4 else 24) * MIB),
        name="forward",
    )(*[blocks_in_vmem(x) for x in arrays])


def piece_blocks(outers, inners, refs):
    singles, groups, forwarded = refs[:outers], refs[outers : outers + inners - 1], refs[outers + inners - 1 :]
    for i in range(outers):
        yield i, singles[i][0]
    for i in range(1, inners):
        yield i * outers, groups[i - 1][0]
        for j in range(1, outers):
            yield i * outers + j, forwarded[j - 1][i - 1]


def gather_kernel(outers, inners, *refs):
    for i, block in piece_blocks(outers, inners, refs[:-1]):
        refs[-1][i] = block


def gather(pieces, chips):
    outers, inners = grid_of(chips)
    width = pieces[0].shape[2]
    vmem = pl.BlockSpec(memory_space=pltpu.VMEM)
    return pl.pallas_call(
        functools.partial(gather_kernel, outers, inners),
        in_specs=[vmem] * len(pieces),
        out_specs=vmem,
        out_shape=blocks_out((chips, CAP, width)),
        compiler_params=pltpu.CompilerParams(vmem_limit_bytes=(4 if chips <= 8 else 24) * MIB),
        name="gather",
    )(*[blocks_in_vmem(x) for x in pieces])


def ffn_kernel(
    deep,
    wide,
    mine_ref,
    other_ref,
    up_ref,
    down_ref,
    gate_ref,
    own_ref,
    lent_ref,
    sems,
    x_ref,
    acc_a,
    acc_b,
    acc_c,
    hid,
    ring,
    *rings,
):
    down_ring = rings[0] if rings else ring
    chips, _, width = mine_ref.shape
    units = gate_ref.shape[1]
    slots = ring.shape[0]
    ups = width // deep
    down_deep = min(deep, units)
    downs_k = units // down_deep
    halves = width // wide
    total = ups + halves * downs_k

    def up_copy(i):
        slot = lax.rem(i, slots)
        row = pl.multiple_of(i * deep, deep)
        return pltpu.make_async_copy(up_ref.at[pl.ds(row, deep)], ring.at[slot], sems.at[slot])

    def down_copy(i):
        slot = lax.rem(i, slots)
        j = i - ups
        row = pl.multiple_of(lax.rem(j, downs_k) * down_deep, down_deep)
        col = pl.multiple_of((j // downs_k) * wide, wide)
        return pltpu.make_async_copy(
            down_ref.at[pl.ds(row, down_deep), pl.ds(col, wide)],
            down_ring.at[slot],
            sems.at[slot],
        )

    def start(i):
        @pl.when(i < ups)
        def _():
            up_copy(i).start()

        @pl.when(jnp.logical_and(i >= ups, i < total))
        def _():
            down_copy(i).start()

    @pl.loop(0, min(slots, total))
    def _(i):
        start(i)

    join_rows(mine_ref, x_ref, 0)
    join_rows(other_ref, x_ref, chips * CAP)
    acc_a[...] = jnp.zeros_like(acc_a)
    acc_b[...] = jnp.zeros_like(acc_b)

    @pl.loop(0, ups)
    def _(i):
        row = pl.multiple_of(i * deep, deep)
        acc_a[...] += jnp.dot(
            x_ref[:, pl.ds(row, deep)],
            gate_ref[pl.ds(row, deep), :],
            preferred_element_type=jnp.float32,
        )

    @pl.loop(0, ups)
    def _(i):
        row = pl.multiple_of(i * deep, deep)
        up_copy(i).wait()
        acc_b[...] += jnp.dot(
            x_ref[:, pl.ds(row, deep)], ring[lax.rem(i, slots)], preferred_element_type=jnp.float32
        )
        start(i + slots)

    gate = acc_a[...]
    hid[...] = (gate / (1.0 + jnp.exp(-gate)) * acc_b[...]).astype(jnp.bfloat16)

    for half in range(halves):
        acc_c[...] = jnp.zeros_like(acc_c)

        @pl.loop(0, downs_k)
        def _(k, half=half):
            i = ups + half * downs_k + k
            slot = lax.rem(i, slots)
            down_copy(i).wait()
            row = pl.multiple_of(k * down_deep, down_deep)
            acc_c[...] += jnp.dot(
                hid[:, pl.ds(row, down_deep)] if downs_k > 1 else hid[...],
                down_ring[slot],
                preferred_element_type=jnp.float32,
            )
            start(i + slots)

        for i in range(chips):
            for part_ref, first in ((own_ref, 0), (lent_ref, chips * CAP)):
                part_ref[i, :, half * wide : (half + 1) * wide] = acc_c[
                    first + i * CAP : first + (i + 1) * CAP, :
                ].astype(jnp.bfloat16)


def ffn(mine, other, gate, up, down):
    chips, _, width = mine.shape
    rows = 2 * chips * CAP
    units = gate.shape[1]
    deep, wide = DEEP, width // 2
    slots = 11 if rows <= 64 else 6
    down_deep = min(deep, units)
    rings = [pltpu.VMEM((slots, deep, units), jnp.bfloat16)]
    if (down_deep, wide) != (deep, units):
        rings.append(pltpu.VMEM((slots, down_deep, wide), jnp.bfloat16))
    vmem = pl.BlockSpec(memory_space=pltpu.VMEM)
    return pl.pallas_call(
        functools.partial(ffn_kernel, deep, wide),
        in_specs=[vmem] * 2 + [pl.BlockSpec(memory_space=pl.ANY)] * 2 + [vmem],
        out_specs=[vmem, vmem],
        out_shape=[blocks_out(mine.shape)] * 2,
        scratch_shapes=[
            pltpu.SemaphoreType.DMA((slots,)),
            pltpu.VMEM((rows, width), jnp.bfloat16),
            pltpu.VMEM((rows, units), jnp.float32),
            pltpu.VMEM((rows, units), jnp.float32),
            pltpu.VMEM((rows, wide), jnp.float32),
            pltpu.VMEM((rows, units), jnp.bfloat16),
            *rings,
        ],
        compiler_params=pltpu.CompilerParams(vmem_limit_bytes=(34 if rows <= 64 else 52) * MIB),
        cost_estimate=pl.CostEstimate(
            flops=6 * rows * width * units,
            bytes_accessed=4 * width * units,
            transcendentals=rows * units,
        ),
        name="ffn",
    )(
        blocks_in_vmem(mine),
        blocks_in_vmem(other),
        in_hbm(up),
        in_hbm(down),
        in_vmem(gate),
    )


def add_kernel(outers, a_ref, b_ref, *outs):
    chips = a_ref.shape[0]
    for i in range(chips):
        block = (a_ref[i].astype(jnp.float32) + b_ref[i].astype(jnp.float32)).astype(jnp.bfloat16)
        if i < outers:
            outs[i][0] = block
        else:
            outs[outers + i // outers - 1][i % outers] = block


def add(a, b):
    chips, _, width = a.shape
    outers, inners = grid_of(chips)
    vmem = pl.BlockSpec(memory_space=pltpu.VMEM)
    return pl.pallas_call(
        functools.partial(add_kernel, outers),
        in_specs=[vmem] * 2,
        out_specs=[vmem] * (outers + inners - 1),
        out_shape=blocks_shapes(chips, width),
        compiler_params=pltpu.CompilerParams(vmem_limit_bytes=16 * MIB),
        name="add",
    )(blocks_in_vmem(a), blocks_in_vmem(b))


def unpack_kernel(outers, inners, target_ref, *refs):
    pieces, (out_ref, rows, out, sems) = refs[:-4], refs[-4:]
    chips = outers * inners
    index = lax.broadcasted_iota(jnp.int32, (rows.shape[0], 1), 0) // CAP
    layout = slot_layout(target_ref[...], partner_chips(chips, index) // (chips // EXP_FL))
    for i, block in piece_blocks(outers, inners, pieces):
        rows[i * CAP : (i + 1) * CAP, :] = block.astype(jnp.float32)
    count = sems.shape[0]
    part = rows.shape[1] // count
    moves = []
    for i in range(count):
        columns = slice(i * part, (i + 1) * part)
        out[:, columns] = lax.dot_general(
            layout,
            rows[:, columns].astype(jnp.bfloat16),
            (((0,), (0,)), ((), ())),
            preferred_element_type=jnp.float32,
        ).astype(jnp.bfloat16)
        moves.append(pltpu.make_async_copy(out.at[:, columns], out_ref.at[:, columns], sems.at[i]))
        moves[-1].start()
    for move in moves:
        move.wait()


def unpack(pieces, target, chips):
    width = pieces[0].shape[2]
    shape = (target.shape[1], width)
    return pl.pallas_call(
        functools.partial(unpack_kernel, *grid_of(chips)),
        in_specs=[pl.BlockSpec(memory_space=pltpu.VMEM)] * (1 + len(pieces)),
        out_specs=pl.BlockSpec(memory_space=pl.ANY),
        out_shape=jax.ShapeDtypeStruct(shape, jnp.bfloat16),
        scratch_shapes=[
            pltpu.VMEM((chips * CAP, width), jnp.float32),
            pltpu.VMEM(shape, jnp.bfloat16),
            pltpu.SemaphoreType.DMA((4,)),
        ],
        compiler_params=pltpu.CompilerParams(vmem_limit_bytes=(16 if chips <= 8 else 32) * MIB),
        name="unpack",
    )(in_vmem(target), *[blocks_in_vmem(x) for x in pieces])


def per_device(tokens, expert_ids, norm_gain, router, gate_weight, up_weight, down_weight):
    devices = lax.axis_size("expert")
    chips = devices // 2
    outers, inners = grid_of(chips)
    ids = expert_ids.reshape(1, -1)
    steps = [2 * inners * i for i in range(1, outers)]

    def send(x, offset):
        return lax.ppermute(x, "expert", [(i, i ^ offset) for i in range(devices)])

    def exchange(blocks):
        singles, groups = blocks[:outers], blocks[outers:]
        near = [send(x, 2 * (i + 1)) for i, x in enumerate(groups)]
        direct = [send(x, step) for x, step in zip(singles[1:], steps)]
        onward = [send(x, step) for x, step in zip(forward(near), steps)]
        return [singles[0], *direct, *near, *onward]

    blocks, target = pack(tokens, ids, norm_gain.reshape(1, -1), router.T, up_weight, chips)
    mine = gather(exchange(blocks), chips)
    own, lent = ffn(mine, send(mine, 1), gate_weight, up_weight, down_weight)
    return unpack(exchange(add(own, send(lent, 1))), target, chips)


def solution(mesh):
    in_specs = (
        P(("groups", "expert"), None),
        P(("groups", "expert")),
        P(),
        P(),
        P(None, "expert"),
        P(None, "expert"),
        P("expert", None),
    )
    out_specs = P(("groups", "expert"), None)
    return jax.shard_map(
        per_device, mesh=mesh, in_specs=in_specs, out_specs=out_specs, check_vma=False
    )
```

```python
import functools
import math

import jax
import jax.numpy as jnp
from jax import lax
from jax.experimental import pallas as pl
from jax.experimental.pallas import tpu as pltpu
from jax.sharding import PartitionSpec as P

EXP_FL = 8
CAP = 4
MIB = 1 << 20
DEEP = 512


def token_rows(ids):
    tokens = ids.shape[1]
    expert = lax.broadcasted_iota(jnp.int32, (EXP_FL, tokens), 0)
    chosen = (jnp.broadcast_to(ids, (EXP_FL, tokens)) == expert).astype(jnp.float32)
    before = lax.broadcasted_iota(jnp.int32, (tokens, tokens), 0) < lax.broadcasted_iota(
        jnp.int32, (tokens, tokens), 1
    )
    earlier = jnp.dot(
        chosen.astype(jnp.bfloat16),
        before.astype(jnp.float32).astype(jnp.bfloat16),
        preferred_element_type=jnp.float32,
    )
    slot = jnp.sum(earlier * chosen, axis=0, keepdims=True).astype(jnp.int32)
    return jnp.where(ids < EXP_FL, ids * CAP + slot, -1)


def slot_layout(target, experts):
    rows, tokens = experts.shape[0], target.shape[1]
    row = experts * CAP + lax.broadcasted_iota(jnp.int32, (rows, 1), 0) % CAP
    return (row == jnp.broadcast_to(target, (rows, tokens))).astype(jnp.float32).astype(jnp.bfloat16)


def grid_of(chips):
    inner = 1 << (int(math.log2(chips)) // 2)
    return chips // inner, inner


def partner_chips(chips, index):
    outers, inners = grid_of(chips)
    here = lax.axis_index("expert") // 2
    return here ^ (index % outers * inners + index // outers)


def in_hbm(x):
    return pltpu.with_memory_space_constraint(x, pltpu.HBM)


def in_vmem(x):
    return pltpu.with_memory_space_constraint(x, pltpu.VMEM)


def blocks_in_vmem(x):
    return in_vmem(x) if x.size <= MIB else x


def blocks_out(shape):
    if math.prod(shape) <= MIB:
        return pltpu.VMEM(shape, jnp.bfloat16)
    return jax.ShapeDtypeStruct(shape, jnp.bfloat16)


def join_rows(blocks_ref, rows_ref, first):
    for i in range(blocks_ref.shape[0]):
        rows_ref[first + i * CAP : first + (i + 1) * CAP, :] = blocks_ref[i].astype(rows_ref.dtype)


def block_refs(outers, inners, refs):
    for i in range(inners):
        for j in range(outers):
            if j == 1:
                yield i * outers + j, refs[1], i
            elif i == 0:
                yield j, refs[j], 0
            else:
                yield i * outers + j, refs[outers + i - 1], max(j - 1, 0)


def blocks_shapes(chips, width):
    outers, inners = grid_of(chips)
    counts = [1, inners] + [1] * (outers - 2) + [outers - 1] * (inners - 1)
    return [blocks_out((count, CAP, width)) for count in counts]


def pack_kernel(outers, *refs):
    ids_ref, tokens_ref, gain_ref, router_ref = refs[:4]
    outs, target_ref = refs[5:-6], refs[-6]
    ids, tokens, gain, router, sems = refs[-5:]
    pairs = ((ids_ref, ids), (tokens_ref, tokens), (gain_ref, gain), (router_ref, router))
    moves = [pltpu.make_async_copy(a, b, sems.at[i]) for i, (a, b) in enumerate(pairs)]
    for move in moves:
        move.start()
    inners = len(outs) - outers + 1
    chips = outers * inners
    rows = chips * CAP
    copies = chips // EXP_FL
    index = lax.broadcasted_iota(jnp.int32, (rows, 1), 0) // CAP
    experts = partner_chips(chips, index) // copies
    moves[0].wait()
    target = token_rows(ids[...])
    target_ref[...] = target
    layout = slot_layout(target, experts)
    moves[3].wait()
    own = lax.broadcasted_iota(jnp.int32, (rows, EXP_FL), 1) == experts
    column = jnp.dot(
        own.astype(jnp.float32).astype(jnp.bfloat16),
        router[...],
        preferred_element_type=jnp.float32,
    )
    moves[1].wait()
    packed = jnp.dot(layout, tokens[...], preferred_element_type=jnp.float32)
    mean_square = jnp.mean(packed * packed, axis=-1, keepdims=True)
    moves[2].wait()
    normed = (packed * lax.rsqrt(mean_square + 1e-05) * gain[...]).astype(jnp.bfloat16)
    normed = normed.astype(jnp.float32)
    logit = jnp.sum(normed * column, axis=-1, keepdims=True)
    routed = normed * jax.nn.sigmoid(logit)
    for i, ref, j in block_refs(outers, inners, outs):
        ref[j] = routed[i * CAP : (i + 1) * CAP].astype(jnp.bfloat16)


def pack(tokens, ids, gain, router_rows, weight, chips):
    width = tokens.shape[1]
    outers, inners = grid_of(chips)
    arrays = (ids, tokens, gain, router_rows)
    outs = pl.pallas_call(
        functools.partial(pack_kernel, outers),
        in_specs=[pl.BlockSpec(memory_space=pl.ANY)] * 5,
        out_specs=[pl.BlockSpec(memory_space=pltpu.VMEM)] * (outers + inners),
        out_shape=blocks_shapes(chips, width) + [pltpu.VMEM(ids.shape, jnp.int32)],
        scratch_shapes=[pltpu.VMEM(x.shape, x.dtype) for x in arrays]
        + [pltpu.SemaphoreType.DMA((4,))],
        compiler_params=pltpu.CompilerParams(vmem_limit_bytes=(12 if chips <= 8 else 40) * MIB),
        name="pack",
    )(*[in_hbm(x) for x in (*arrays, weight)])
    return outs[:-1], outs[-1]


def forward_kernel(first, groups, *refs):
    for i, out_ref in enumerate(refs[groups:]):
        for j in range(groups):
            out_ref[j] = refs[j][first + i]


def forward(arrays):
    count, _, width = arrays[0].shape
    vmem = pl.BlockSpec(memory_space=pltpu.VMEM)
    return pl.pallas_call(
        functools.partial(forward_kernel, 1, len(arrays)),
        in_specs=[vmem] * len(arrays),
        out_specs=[vmem] * (count - 1),
        out_shape=[blocks_out((len(arrays), CAP, width))] * (count - 1),
        compiler_params=pltpu.CompilerParams(vmem_limit_bytes=(4 if count <= 4 else 24) * MIB),
        name="forward",
    )(*[blocks_in_vmem(x) for x in arrays])


def piece_blocks(outers, inners, refs):
    direct, near = refs[:outers], refs[outers : outers + inners - 1]
    onward, beside = refs[outers + inners - 1 : 1 - inners], refs[1 - inners :]
    for i in range(inners):
        for j in range(outers):
            if i == 0:
                block = direct[j][0]
            elif j == 0:
                block = near[i - 1][0]
            elif j == 1:
                block = beside[i - 1][0]
            else:
                block = onward[j - 2][i - 1]
            yield i * outers + j, block


def gather_kernel(outers, inners, *refs):
    for i, block in piece_blocks(outers, inners, refs[:-1]):
        refs[-1][i] = block


def gather(pieces, chips):
    outers, inners = grid_of(chips)
    width = pieces[0].shape[2]
    vmem = pl.BlockSpec(memory_space=pltpu.VMEM)
    return pl.pallas_call(
        functools.partial(gather_kernel, outers, inners),
        in_specs=[vmem] * len(pieces),
        out_specs=vmem,
        out_shape=blocks_out((chips, CAP, width)),
        compiler_params=pltpu.CompilerParams(vmem_limit_bytes=(4 if chips <= 8 else 24) * MIB),
        name="gather",
    )(*[blocks_in_vmem(x) for x in pieces])


def ffn_kernel(
    deep,
    wide,
    mine_ref,
    other_ref,
    up_ref,
    down_ref,
    gate_ref,
    own_ref,
    lent_ref,
    sems,
    x_ref,
    acc_a,
    acc_b,
    acc_c,
    hid,
    ring,
    *rings,
):
    down_ring = rings[0] if rings else ring
    chips, _, width = mine_ref.shape
    units = gate_ref.shape[1]
    slots = ring.shape[0]
    ups = width // deep
    down_deep = min(deep, units)
    downs_k = units // down_deep
    halves = width // wide
    total = ups + halves * downs_k

    def up_copy(i):
        slot = lax.rem(i, slots)
        row = pl.multiple_of(i * deep, deep)
        return pltpu.make_async_copy(up_ref.at[pl.ds(row, deep)], ring.at[slot], sems.at[slot])

    def down_copy(i):
        slot = lax.rem(i, slots)
        j = i - ups
        row = pl.multiple_of(lax.rem(j, downs_k) * down_deep, down_deep)
        col = pl.multiple_of((j // downs_k) * wide, wide)
        return pltpu.make_async_copy(
            down_ref.at[pl.ds(row, down_deep), pl.ds(col, wide)],
            down_ring.at[slot],
            sems.at[slot],
        )

    def start(i):
        @pl.when(i < ups)
        def _():
            up_copy(i).start()

        @pl.when(jnp.logical_and(i >= ups, i < total))
        def _():
            down_copy(i).start()

    @pl.loop(0, min(slots, total))
    def _(i):
        start(i)

    join_rows(mine_ref, x_ref, 0)
    join_rows(other_ref, x_ref, chips * CAP)
    acc_a[...] = jnp.zeros_like(acc_a)
    acc_b[...] = jnp.zeros_like(acc_b)

    @pl.loop(0, ups)
    def _(i):
        row = pl.multiple_of(i * deep, deep)
        acc_a[...] += jnp.dot(
            x_ref[:, pl.ds(row, deep)],
            gate_ref[pl.ds(row, deep), :],
            preferred_element_type=jnp.float32,
        )

    @pl.loop(0, ups)
    def _(i):
        row = pl.multiple_of(i * deep, deep)
        up_copy(i).wait()
        acc_b[...] += jnp.dot(
            x_ref[:, pl.ds(row, deep)], ring[lax.rem(i, slots)], preferred_element_type=jnp.float32
        )
        start(i + slots)

    gate = acc_a[...]
    hid[...] = (gate / (1.0 + jnp.exp(-gate)) * acc_b[...]).astype(jnp.bfloat16)

    for half in range(halves):
        acc_c[...] = jnp.zeros_like(acc_c)

        @pl.loop(0, downs_k)
        def _(k, half=half):
            i = ups + half * downs_k + k
            slot = lax.rem(i, slots)
            down_copy(i).wait()
            row = pl.multiple_of(k * down_deep, down_deep)
            acc_c[...] += jnp.dot(
                hid[:, pl.ds(row, down_deep)] if downs_k > 1 else hid[...],
                down_ring[slot],
                preferred_element_type=jnp.float32,
            )
            start(i + slots)

        for i in range(chips):
            for part_ref, first in ((own_ref, 0), (lent_ref, chips * CAP)):
                part_ref[i, :, half * wide : (half + 1) * wide] = acc_c[
                    first + i * CAP : first + (i + 1) * CAP, :
                ].astype(jnp.bfloat16)


def ffn(mine, other, gate, up, down):
    chips, _, width = mine.shape
    rows = 2 * chips * CAP
    units = gate.shape[1]
    deep, wide = DEEP, width // 2
    slots = 11 if rows <= 64 else 6
    down_deep = min(deep, units)
    rings = [pltpu.VMEM((slots, deep, units), jnp.bfloat16)]
    if (down_deep, wide) != (deep, units):
        rings.append(pltpu.VMEM((slots, down_deep, wide), jnp.bfloat16))
    vmem = pl.BlockSpec(memory_space=pltpu.VMEM)
    return pl.pallas_call(
        functools.partial(ffn_kernel, deep, wide),
        in_specs=[vmem] * 2 + [pl.BlockSpec(memory_space=pl.ANY)] * 2 + [vmem],
        out_specs=[vmem, vmem],
        out_shape=[blocks_out(mine.shape)] * 2,
        scratch_shapes=[
            pltpu.SemaphoreType.DMA((slots,)),
            pltpu.VMEM((rows, width), jnp.bfloat16),
            pltpu.VMEM((rows, units), jnp.float32),
            pltpu.VMEM((rows, units), jnp.float32),
            pltpu.VMEM((rows, wide), jnp.float32),
            pltpu.VMEM((rows, units), jnp.bfloat16),
            *rings,
        ],
        compiler_params=pltpu.CompilerParams(vmem_limit_bytes=(34 if rows <= 64 else 52) * MIB),
        cost_estimate=pl.CostEstimate(
            flops=6 * rows * width * units,
            bytes_accessed=4 * width * units,
            transcendentals=rows * units,
        ),
        name="ffn",
    )(
        blocks_in_vmem(mine),
        blocks_in_vmem(other),
        in_hbm(up),
        in_hbm(down),
        in_vmem(gate),
    )


def add_kernel(outers, inners, a_ref, b_ref, *outs):
    for i, ref, j in block_refs(outers, inners, outs):
        ref[j] = (a_ref[i].astype(jnp.float32) + b_ref[i].astype(jnp.float32)).astype(jnp.bfloat16)


def add(a, b):
    chips, _, width = a.shape
    outers, inners = grid_of(chips)
    vmem = pl.BlockSpec(memory_space=pltpu.VMEM)
    return pl.pallas_call(
        functools.partial(add_kernel, outers, inners),
        in_specs=[vmem] * 2,
        out_specs=[vmem] * (outers + inners - 1),
        out_shape=blocks_shapes(chips, width),
        compiler_params=pltpu.CompilerParams(vmem_limit_bytes=16 * MIB),
        name="add",
    )(blocks_in_vmem(a), blocks_in_vmem(b))


def unpack_kernel(outers, inners, target_ref, *refs):
    pieces, (out_ref, rows, out, sems) = refs[:-4], refs[-4:]
    chips = outers * inners
    index = lax.broadcasted_iota(jnp.int32, (rows.shape[0], 1), 0) // CAP
    layout = slot_layout(target_ref[...], partner_chips(chips, index) // (chips // EXP_FL))
    for i, block in piece_blocks(outers, inners, pieces):
        rows[i * CAP : (i + 1) * CAP, :] = block.astype(jnp.float32)
    count = sems.shape[0]
    part = rows.shape[1] // count
    moves = []
    for i in range(count):
        columns = slice(i * part, (i + 1) * part)
        out[:, columns] = lax.dot_general(
            layout,
            rows[:, columns].astype(jnp.bfloat16),
            (((0,), (0,)), ((), ())),
            preferred_element_type=jnp.float32,
        ).astype(jnp.bfloat16)
        moves.append(pltpu.make_async_copy(out.at[:, columns], out_ref.at[:, columns], sems.at[i]))
        moves[-1].start()
    for move in moves:
        move.wait()


def unpack(pieces, target, chips):
    width = pieces[0].shape[2]
    shape = (target.shape[1], width)
    return pl.pallas_call(
        functools.partial(unpack_kernel, *grid_of(chips)),
        in_specs=[pl.BlockSpec(memory_space=pltpu.VMEM)] * (1 + len(pieces)),
        out_specs=pl.BlockSpec(memory_space=pl.ANY),
        out_shape=jax.ShapeDtypeStruct(shape, jnp.bfloat16),
        scratch_shapes=[
            pltpu.VMEM((chips * CAP, width), jnp.float32),
            pltpu.VMEM(shape, jnp.bfloat16),
            pltpu.SemaphoreType.DMA((4,)),
        ],
        compiler_params=pltpu.CompilerParams(vmem_limit_bytes=(16 if chips <= 8 else 32) * MIB),
        name="unpack",
    )(in_vmem(target), *[blocks_in_vmem(x) for x in pieces])


def per_device(tokens, expert_ids, norm_gain, router, gate_weight, up_weight, down_weight):
    devices = lax.axis_size("expert")
    chips = devices // 2
    outers, inners = grid_of(chips)
    ids = expert_ids.reshape(1, -1)
    steps = [2 * inners * i for i in range(1, outers)]

    def send(x, offset):
        return lax.ppermute(x, "expert", [(i, i ^ offset) for i in range(devices)])

    def exchange(blocks):
        near = [send(x, 2 * (i + 1)) for i, x in enumerate(blocks[outers:])]
        direct = [send(x, step) for x, step in zip(blocks[1:outers], steps)]
        onward = [send(x, step) for x, step in zip(forward(near), steps[1:])]
        beside = [send(x, 2 * (i + 1)) for i, x in enumerate(forward(direct[:1]))]
        return [blocks[0], *direct, *near, *onward, *beside]

    blocks, target = pack(tokens, ids, norm_gain.reshape(1, -1), router.T, up_weight, chips)
    mine = gather(exchange(blocks), chips)
    own, lent = ffn(mine, send(mine, 1), gate_weight, up_weight, down_weight)
    return unpack(exchange(add(own, send(lent, 1))), target, chips)


def solution(mesh):
    in_specs = (
        P(("groups", "expert"), None),
        P(("groups", "expert")),
        P(),
        P(),
        P(None, "expert"),
        P(None, "expert"),
        P("expert", None),
    )
    out_specs = P(("groups", "expert"), None)
    return jax.shard_map(
        per_device, mesh=mesh, in_specs=in_specs, out_specs=out_specs, check_vma=False
    )
```

```python
import functools
import math

import jax
import jax.numpy as jnp
from jax import lax
from jax.experimental import pallas as pl
from jax.experimental.pallas import tpu as pltpu
from jax.sharding import PartitionSpec as P

EXP_FL = 8
CAP = 4
MIB = 1 << 20
DEEP = 512


def token_rows(ids):
    tokens = ids.shape[1]
    expert = lax.broadcasted_iota(jnp.int32, (EXP_FL, tokens), 0)
    chosen = (jnp.broadcast_to(ids, (EXP_FL, tokens)) == expert).astype(jnp.float32)
    before = lax.broadcasted_iota(jnp.int32, (tokens, tokens), 0) < lax.broadcasted_iota(
        jnp.int32, (tokens, tokens), 1
    )
    earlier = jnp.dot(
        chosen.astype(jnp.bfloat16),
        before.astype(jnp.float32).astype(jnp.bfloat16),
        preferred_element_type=jnp.float32,
    )
    slot = jnp.sum(earlier * chosen, axis=0, keepdims=True).astype(jnp.int32)
    return jnp.where(ids < EXP_FL, ids * CAP + slot, -1)


def slot_layout(target, experts):
    rows, tokens = experts.shape[0], target.shape[1]
    row = experts * CAP + lax.broadcasted_iota(jnp.int32, (rows, 1), 0) % CAP
    return (row == jnp.broadcast_to(target, (rows, tokens))).astype(jnp.float32).astype(jnp.bfloat16)


def grid_of(chips):
    inner = 1 << (int(math.log2(chips)) // 2)
    return chips // inner, inner


def partner_chips(chips, index):
    outers, inners = grid_of(chips)
    here = lax.axis_index("expert") // 2
    return here ^ (index % outers * inners + index // outers)


def in_hbm(x):
    return pltpu.with_memory_space_constraint(x, pltpu.HBM)


def in_vmem(x):
    return pltpu.with_memory_space_constraint(x, pltpu.VMEM)


def blocks_in_vmem(x):
    return in_vmem(x) if x.size <= MIB else x


def blocks_out(shape):
    if math.prod(shape) <= MIB:
        return pltpu.VMEM(shape, jnp.bfloat16)
    return jax.ShapeDtypeStruct(shape, jnp.bfloat16)


def join_rows(blocks_ref, rows_ref, first):
    for i in range(blocks_ref.shape[0]):
        rows_ref[first + i * CAP : first + (i + 1) * CAP, :] = blocks_ref[i].astype(rows_ref.dtype)


def block_refs(outers, inners, refs):
    for i in range(inners):
        for j in range(outers):
            if j == 1:
                yield i * outers + j, refs[1], i
            elif i == 0:
                yield j, refs[j], 0
            else:
                yield i * outers + j, refs[outers + i - 1], max(j - 1, 0)


def blocks_shapes(chips, width):
    outers, inners = grid_of(chips)
    counts = [1, inners] + [1] * (outers - 2) + [outers - 1] * (inners - 1)
    return [blocks_out((count, CAP, width)) for count in counts]


def pack_kernel(outers, *refs):
    ids_ref, tokens_ref, gain_ref, router_ref = refs[:4]
    outs, target_ref = refs[5:-6], refs[-6]
    ids, tokens, gain, router, sems = refs[-5:]
    pairs = ((ids_ref, ids), (tokens_ref, tokens), (gain_ref, gain), (router_ref, router))
    moves = [pltpu.make_async_copy(a, b, sems.at[i]) for i, (a, b) in enumerate(pairs)]
    for move in moves:
        move.start()
    inners = len(outs) - outers + 1
    chips = outers * inners
    rows = chips * CAP
    copies = chips // EXP_FL
    index = lax.broadcasted_iota(jnp.int32, (rows, 1), 0) // CAP
    experts = partner_chips(chips, index) // copies
    moves[0].wait()
    target = token_rows(ids[...])
    target_ref[...] = target
    layout = slot_layout(target, experts)
    moves[3].wait()
    own = lax.broadcasted_iota(jnp.int32, (rows, EXP_FL), 1) == experts
    column = jnp.dot(
        own.astype(jnp.float32).astype(jnp.bfloat16),
        router[...],
        preferred_element_type=jnp.float32,
    )
    moves[1].wait()
    packed = jnp.dot(layout, tokens[...], preferred_element_type=jnp.float32)
    mean_square = jnp.mean(packed * packed, axis=-1, keepdims=True)
    moves[2].wait()
    normed = (packed * lax.rsqrt(mean_square + 1e-05) * gain[...]).astype(jnp.bfloat16)
    normed = normed.astype(jnp.float32)
    logit = jnp.sum(normed * column, axis=-1, keepdims=True)
    routed = normed * jax.nn.sigmoid(logit)
    for i, ref, j in block_refs(outers, inners, outs):
        ref[j] = routed[i * CAP : (i + 1) * CAP].astype(jnp.bfloat16)


def pack(tokens, ids, gain, router_rows, weight, chips):
    width = tokens.shape[1]
    outers, inners = grid_of(chips)
    arrays = (ids, tokens, gain, router_rows)
    outs = pl.pallas_call(
        functools.partial(pack_kernel, outers),
        in_specs=[pl.BlockSpec(memory_space=pl.ANY)] * 5,
        out_specs=[pl.BlockSpec(memory_space=pltpu.VMEM)] * (outers + inners),
        out_shape=blocks_shapes(chips, width) + [pltpu.VMEM(ids.shape, jnp.int32)],
        scratch_shapes=[pltpu.VMEM(x.shape, x.dtype) for x in arrays]
        + [pltpu.SemaphoreType.DMA((4,))],
        compiler_params=pltpu.CompilerParams(vmem_limit_bytes=(12 if chips <= 8 else 40) * MIB),
        name="pack",
    )(*[in_hbm(x) for x in (*arrays, weight)])
    return outs[:-1], outs[-1]


def forward_kernel(first, groups, *refs):
    for i, out_ref in enumerate(refs[groups:]):
        for j in range(groups):
            out_ref[j] = refs[j][first + i]


def forward(arrays):
    count, _, width = arrays[0].shape
    vmem = pl.BlockSpec(memory_space=pltpu.VMEM)
    return pl.pallas_call(
        functools.partial(forward_kernel, 1, len(arrays)),
        in_specs=[vmem] * len(arrays),
        out_specs=[vmem] * (count - 1),
        out_shape=[blocks_out((len(arrays), CAP, width))] * (count - 1),
        compiler_params=pltpu.CompilerParams(vmem_limit_bytes=(4 if count <= 4 else 24) * MIB),
        name="forward",
    )(*[blocks_in_vmem(x) for x in arrays])


def piece_blocks(outers, inners, refs):
    onward, beside = refs[: outers - 2], refs[outers - 2 : outers + inners - 3]
    rest = refs[outers + inners - 3 :]
    direct, near = [rest[-1], *rest[: outers - 1][::-1]], rest[outers - 1 : -1]
    for i in range(inners):
        for j in range(outers):
            if i == 0:
                block = direct[j][0]
            elif j == 0:
                block = near[i - 1][0]
            elif j == 1:
                block = beside[i - 1][0]
            else:
                block = onward[j - 2][i - 1]
            yield i * outers + j, block


def gather_kernel(outers, inners, *refs):
    for i, block in piece_blocks(outers, inners, refs[:-1]):
        refs[-1][i] = block


def gather(pieces, chips):
    outers, inners = grid_of(chips)
    width = pieces[0].shape[2]
    vmem = pl.BlockSpec(memory_space=pltpu.VMEM)
    return pl.pallas_call(
        functools.partial(gather_kernel, outers, inners),
        in_specs=[vmem] * len(pieces),
        out_specs=vmem,
        out_shape=blocks_out((chips, CAP, width)),
        compiler_params=pltpu.CompilerParams(vmem_limit_bytes=(4 if chips <= 8 else 24) * MIB),
        name="gather",
    )(*[blocks_in_vmem(x) for x in pieces])


def ffn_kernel(
    deep,
    wide,
    mine_ref,
    other_ref,
    up_ref,
    down_ref,
    gate_ref,
    own_ref,
    lent_ref,
    sems,
    x_ref,
    acc_a,
    acc_b,
    acc_c,
    hid,
    ring,
    *rings,
):
    down_ring = rings[0] if rings else ring
    chips, _, width = mine_ref.shape
    units = gate_ref.shape[1]
    slots = ring.shape[0]
    ups = width // deep
    down_deep = min(deep, units)
    downs_k = units // down_deep
    halves = width // wide
    total = ups + halves * downs_k

    def up_copy(i):
        slot = lax.rem(i, slots)
        row = pl.multiple_of(i * deep, deep)
        return pltpu.make_async_copy(up_ref.at[pl.ds(row, deep)], ring.at[slot], sems.at[slot])

    def down_copy(i):
        slot = lax.rem(i, slots)
        j = i - ups
        row = pl.multiple_of(lax.rem(j, downs_k) * down_deep, down_deep)
        col = pl.multiple_of((j // downs_k) * wide, wide)
        return pltpu.make_async_copy(
            down_ref.at[pl.ds(row, down_deep), pl.ds(col, wide)],
            down_ring.at[slot],
            sems.at[slot],
        )

    def start(i):
        @pl.when(i < ups)
        def _():
            up_copy(i).start()

        @pl.when(jnp.logical_and(i >= ups, i < total))
        def _():
            down_copy(i).start()

    @pl.loop(0, min(slots, total))
    def _(i):
        start(i)

    join_rows(mine_ref, x_ref, 0)
    join_rows(other_ref, x_ref, chips * CAP)
    acc_a[...] = jnp.zeros_like(acc_a)
    acc_b[...] = jnp.zeros_like(acc_b)

    @pl.loop(0, ups)
    def _(i):
        row = pl.multiple_of(i * deep, deep)
        acc_a[...] += jnp.dot(
            x_ref[:, pl.ds(row, deep)],
            gate_ref[pl.ds(row, deep), :],
            preferred_element_type=jnp.float32,
        )

    @pl.loop(0, ups)
    def _(i):
        row = pl.multiple_of(i * deep, deep)
        up_copy(i).wait()
        acc_b[...] += jnp.dot(
            x_ref[:, pl.ds(row, deep)], ring[lax.rem(i, slots)], preferred_element_type=jnp.float32
        )
        start(i + slots)

    gate = acc_a[...]
    hid[...] = (gate / (1.0 + jnp.exp(-gate)) * acc_b[...]).astype(jnp.bfloat16)

    for half in range(halves):
        acc_c[...] = jnp.zeros_like(acc_c)

        @pl.loop(0, downs_k)
        def _(k, half=half):
            i = ups + half * downs_k + k
            slot = lax.rem(i, slots)
            down_copy(i).wait()
            row = pl.multiple_of(k * down_deep, down_deep)
            acc_c[...] += jnp.dot(
                hid[:, pl.ds(row, down_deep)] if downs_k > 1 else hid[...],
                down_ring[slot],
                preferred_element_type=jnp.float32,
            )
            start(i + slots)

        for i in range(chips):
            for part_ref, first in ((own_ref, 0), (lent_ref, chips * CAP)):
                part_ref[i, :, half * wide : (half + 1) * wide] = acc_c[
                    first + i * CAP : first + (i + 1) * CAP, :
                ].astype(jnp.bfloat16)


def ffn(mine, other, gate, up, down):
    chips, _, width = mine.shape
    rows = 2 * chips * CAP
    units = gate.shape[1]
    deep, wide = DEEP, width // 2
    slots = 11 if rows <= 64 else 6
    down_deep = min(deep, units)
    rings = [pltpu.VMEM((slots, deep, units), jnp.bfloat16)]
    if (down_deep, wide) != (deep, units):
        rings.append(pltpu.VMEM((slots, down_deep, wide), jnp.bfloat16))
    vmem = pl.BlockSpec(memory_space=pltpu.VMEM)
    return pl.pallas_call(
        functools.partial(ffn_kernel, deep, wide),
        in_specs=[vmem] * 2 + [pl.BlockSpec(memory_space=pl.ANY)] * 2 + [vmem],
        out_specs=[vmem, vmem],
        out_shape=[blocks_out(mine.shape)] * 2,
        scratch_shapes=[
            pltpu.SemaphoreType.DMA((slots,)),
            pltpu.VMEM((rows, width), jnp.bfloat16),
            pltpu.VMEM((rows, units), jnp.float32),
            pltpu.VMEM((rows, units), jnp.float32),
            pltpu.VMEM((rows, wide), jnp.float32),
            pltpu.VMEM((rows, units), jnp.bfloat16),
            *rings,
        ],
        compiler_params=pltpu.CompilerParams(vmem_limit_bytes=(34 if rows <= 64 else 52) * MIB),
        cost_estimate=pl.CostEstimate(
            flops=6 * rows * width * units,
            bytes_accessed=4 * width * units,
            transcendentals=rows * units,
        ),
        name="ffn",
    )(
        blocks_in_vmem(mine),
        blocks_in_vmem(other),
        in_hbm(up),
        in_hbm(down),
        in_vmem(gate),
    )


def add_kernel(outers, inners, a_ref, b_ref, *outs):
    for i, ref, j in block_refs(outers, inners, outs):
        ref[j] = (a_ref[i].astype(jnp.float32) + b_ref[i].astype(jnp.float32)).astype(jnp.bfloat16)


def add(a, b):
    chips, _, width = a.shape
    outers, inners = grid_of(chips)
    vmem = pl.BlockSpec(memory_space=pltpu.VMEM)
    return pl.pallas_call(
        functools.partial(add_kernel, outers, inners),
        in_specs=[vmem] * 2,
        out_specs=[vmem] * (outers + inners - 1),
        out_shape=blocks_shapes(chips, width),
        compiler_params=pltpu.CompilerParams(vmem_limit_bytes=16 * MIB),
        name="add",
    )(blocks_in_vmem(a), blocks_in_vmem(b))


def unpack_kernel(outers, inners, target_ref, *refs):
    pieces, (out_ref, rows, out, sems) = refs[:-4], refs[-4:]
    chips = outers * inners
    index = lax.broadcasted_iota(jnp.int32, (rows.shape[0], 1), 0) // CAP
    layout = slot_layout(target_ref[...], partner_chips(chips, index) // (chips // EXP_FL))
    for i, block in piece_blocks(outers, inners, pieces):
        rows[i * CAP : (i + 1) * CAP, :] = block.astype(jnp.float32)
    count = sems.shape[0]
    part = rows.shape[1] // count
    moves = []
    for i in range(count):
        columns = slice(i * part, (i + 1) * part)
        out[:, columns] = lax.dot_general(
            layout,
            rows[:, columns].astype(jnp.bfloat16),
            (((0,), (0,)), ((), ())),
            preferred_element_type=jnp.float32,
        ).astype(jnp.bfloat16)
        moves.append(pltpu.make_async_copy(out.at[:, columns], out_ref.at[:, columns], sems.at[i]))
        moves[-1].start()
    for move in moves:
        move.wait()


def unpack(pieces, target, chips):
    width = pieces[0].shape[2]
    shape = (target.shape[1], width)
    return pl.pallas_call(
        functools.partial(unpack_kernel, *grid_of(chips)),
        in_specs=[pl.BlockSpec(memory_space=pltpu.VMEM)] * (1 + len(pieces)),
        out_specs=pl.BlockSpec(memory_space=pl.ANY),
        out_shape=jax.ShapeDtypeStruct(shape, jnp.bfloat16),
        scratch_shapes=[
            pltpu.VMEM((chips * CAP, width), jnp.float32),
            pltpu.VMEM(shape, jnp.bfloat16),
            pltpu.SemaphoreType.DMA((4,)),
        ],
        compiler_params=pltpu.CompilerParams(vmem_limit_bytes=(16 if chips <= 8 else 32) * MIB),
        name="unpack",
    )(in_vmem(target), *[blocks_in_vmem(x) for x in pieces])


def per_device(tokens, expert_ids, norm_gain, router, gate_weight, up_weight, down_weight):
    devices = lax.axis_size("expert")
    chips = devices // 2
    outers, inners = grid_of(chips)
    ids = expert_ids.reshape(1, -1)
    steps = [2 * inners * i for i in range(1, outers)]

    def send(x, offset):
        return lax.ppermute(x, "expert", [(i, i ^ offset) for i in range(devices)])

    def exchange(blocks):
        near = [send(x, 2 * (i + 1)) for i, x in enumerate(blocks[outers:])]
        direct = [send(x, step) for x, step in zip(blocks[1:outers], steps)]
        onward = [send(x, step) for x, step in zip(forward(near), steps[1:])]
        beside = [send(x, 2 * (i + 1)) for i, x in enumerate(forward(direct[:1]))]
        return [*onward, *beside, *direct[::-1], *near, blocks[0]]

    blocks, target = pack(tokens, ids, norm_gain.reshape(1, -1), router.T, up_weight, chips)
    mine = gather(exchange(blocks), chips)
    own, lent = ffn(mine, send(mine, 1), gate_weight, up_weight, down_weight)
    return unpack(exchange(add(own, send(lent, 1))), target, chips)


def solution(mesh):
    in_specs = (
        P(("groups", "expert"), None),
        P(("groups", "expert")),
        P(),
        P(),
        P(None, "expert"),
        P(None, "expert"),
        P("expert", None),
    )
    out_specs = P(("groups", "expert"), None)
    return jax.shard_map(
        per_device, mesh=mesh, in_specs=in_specs, out_specs=out_specs, check_vma=False
    )
```

```python
import functools
import math

import jax
import jax.numpy as jnp
from jax import lax
from jax.experimental import pallas as pl
from jax.experimental.pallas import tpu as pltpu
from jax.sharding import PartitionSpec as P

EXP_FL = 8
CAP = 4
MIB = 1 << 20
DEEP = 512


def token_rows(ids):
    tokens = ids.shape[1]
    expert = lax.broadcasted_iota(jnp.int32, (EXP_FL, tokens), 0)
    chosen = (jnp.broadcast_to(ids, (EXP_FL, tokens)) == expert).astype(jnp.float32)
    before = lax.broadcasted_iota(jnp.int32, (tokens, tokens), 0) < lax.broadcasted_iota(
        jnp.int32, (tokens, tokens), 1
    )
    earlier = jnp.dot(
        chosen.astype(jnp.bfloat16),
        before.astype(jnp.float32).astype(jnp.bfloat16),
        preferred_element_type=jnp.float32,
    )
    slot = jnp.sum(earlier * chosen, axis=0, keepdims=True).astype(jnp.int32)
    return jnp.where(ids < EXP_FL, ids * CAP + slot, -1)


def slot_layout(target, experts):
    rows, tokens = experts.shape[0], target.shape[1]
    row = experts * CAP + lax.broadcasted_iota(jnp.int32, (rows, 1), 0) % CAP
    return (row == jnp.broadcast_to(target, (rows, tokens))).astype(jnp.float32).astype(jnp.bfloat16)


def grid_of(chips):
    inner = 1 << (int(math.log2(chips)) // 2)
    return chips // inner, inner


def partner_chips(chips, index):
    outers, inners = grid_of(chips)
    here = lax.axis_index("expert") // 2
    return here ^ (index % outers * inners + index // outers)


def in_hbm(x):
    return pltpu.with_memory_space_constraint(x, pltpu.HBM)


def in_vmem(x):
    return pltpu.with_memory_space_constraint(x, pltpu.VMEM)


def blocks_in_vmem(x):
    return in_vmem(x) if x.size <= MIB else x


def blocks_out(shape):
    if math.prod(shape) <= MIB:
        return pltpu.VMEM(shape, jnp.bfloat16)
    return jax.ShapeDtypeStruct(shape, jnp.bfloat16)


def join_rows(blocks_ref, rows_ref, first):
    for i in range(blocks_ref.shape[0]):
        rows_ref[first + i * CAP : first + (i + 1) * CAP, :] = blocks_ref[i].astype(rows_ref.dtype)


def block_refs(outers, inners, refs):
    for i in range(inners):
        for j in range(outers):
            if j == 1:
                yield i * outers + j, refs[1], i
            elif i == 0:
                yield j, refs[j], 0
            else:
                yield i * outers + j, refs[outers + i - 1], max(j - 1, 0)


def blocks_shapes(chips, width):
    outers, inners = grid_of(chips)
    counts = [1, inners] + [1] * (outers - 2) + [outers - 1] * (inners - 1)
    return [blocks_out((count, CAP, width)) for count in counts]


def pack_kernel(outers, *refs):
    ids_ref, tokens_ref, gain_ref, router_ref = refs[:4]
    outs, target_ref = refs[5:-6], refs[-6]
    ids, tokens, gain, router, sems = refs[-5:]
    pairs = ((ids_ref, ids), (tokens_ref, tokens), (gain_ref, gain), (router_ref, router))
    moves = [pltpu.make_async_copy(a, b, sems.at[i]) for i, (a, b) in enumerate(pairs)]
    for move in moves:
        move.start()
    inners = len(outs) - outers + 1
    chips = outers * inners
    rows = chips * CAP
    copies = chips // EXP_FL
    index = lax.broadcasted_iota(jnp.int32, (rows, 1), 0) // CAP
    experts = partner_chips(chips, index) // copies
    moves[0].wait()
    target = token_rows(ids[...])
    target_ref[...] = target
    layout = slot_layout(target, experts)
    moves[3].wait()
    own = lax.broadcasted_iota(jnp.int32, (rows, EXP_FL), 1) == experts
    column = jnp.dot(
        own.astype(jnp.float32).astype(jnp.bfloat16),
        router[...],
        preferred_element_type=jnp.float32,
    )
    moves[1].wait()
    packed = jnp.dot(layout, tokens[...], preferred_element_type=jnp.float32)
    mean_square = jnp.mean(packed * packed, axis=-1, keepdims=True)
    moves[2].wait()
    normed = (packed * lax.rsqrt(mean_square + 1e-05) * gain[...]).astype(jnp.bfloat16)
    normed = normed.astype(jnp.float32)
    logit = jnp.sum(normed * column, axis=-1, keepdims=True)
    routed = normed * jax.nn.sigmoid(logit)
    for i, ref, j in block_refs(outers, inners, outs):
        ref[j] = routed[i * CAP : (i + 1) * CAP].astype(jnp.bfloat16)


def pack(tokens, ids, gain, router_rows, weight, chips):
    width = tokens.shape[1]
    outers, inners = grid_of(chips)
    arrays = (ids, tokens, gain, router_rows)
    outs = pl.pallas_call(
        functools.partial(pack_kernel, outers),
        in_specs=[pl.BlockSpec(memory_space=pl.ANY)] * 5,
        out_specs=[pl.BlockSpec(memory_space=pltpu.VMEM)] * (outers + inners),
        out_shape=blocks_shapes(chips, width) + [pltpu.VMEM(ids.shape, jnp.int32)],
        scratch_shapes=[pltpu.VMEM(x.shape, x.dtype) for x in arrays]
        + [pltpu.SemaphoreType.DMA((4,))],
        compiler_params=pltpu.CompilerParams(vmem_limit_bytes=(12 if chips <= 8 else 40) * MIB),
        name="pack",
    )(*[in_hbm(x) for x in (*arrays, weight)])
    return outs[:-1], outs[-1]


def forward_kernel(first, groups, *refs):
    for i, out_ref in enumerate(refs[groups:]):
        for j in range(groups):
            out_ref[j] = refs[j][first + i]


def forward(arrays):
    count, _, width = arrays[0].shape
    vmem = pl.BlockSpec(memory_space=pltpu.VMEM)
    return pl.pallas_call(
        functools.partial(forward_kernel, 1, len(arrays)),
        in_specs=[vmem] * len(arrays),
        out_specs=[vmem] * (count - 1),
        out_shape=[blocks_out((len(arrays), CAP, width))] * (count - 1),
        compiler_params=pltpu.CompilerParams(vmem_limit_bytes=(4 if count <= 4 else 24) * MIB),
        name="forward",
    )(*[blocks_in_vmem(x) for x in arrays])


def piece_blocks(outers, inners, refs):
    onward, beside = refs[: outers - 2], refs[outers - 2 : outers + inners - 3]
    rest = refs[outers + inners - 3 :]
    direct, near = [rest[-1], *rest[: outers - 1][::-1]], rest[outers - 1 : -1]
    for i in range(inners):
        for j in range(outers):
            if i == 0:
                block = direct[j][0]
            elif j == 0:
                block = near[i - 1][0]
            elif j == 1:
                block = beside[i - 1][0]
            else:
                block = onward[j - 2][i - 1]
            yield i * outers + j, block


def gather_kernel(outers, inners, *refs):
    for i, block in piece_blocks(outers, inners, refs[:-1]):
        refs[-1][i] = block


def gather(pieces, chips):
    outers, inners = grid_of(chips)
    width = pieces[0].shape[2]
    vmem = pl.BlockSpec(memory_space=pltpu.VMEM)
    return pl.pallas_call(
        functools.partial(gather_kernel, outers, inners),
        in_specs=[vmem] * len(pieces),
        out_specs=vmem,
        out_shape=blocks_out((chips, CAP, width)),
        compiler_params=pltpu.CompilerParams(vmem_limit_bytes=(4 if chips <= 8 else 24) * MIB),
        name="gather",
    )(*[blocks_in_vmem(x) for x in pieces])


def ffn_kernel(
    deep,
    wide,
    mine_ref,
    other_ref,
    up_ref,
    down_ref,
    gate_ref,
    own_ref,
    lent_ref,
    sems,
    x_ref,
    acc_a,
    acc_b,
    acc_c,
    hid,
    ring,
    *rings,
):
    down_ring = rings[0] if rings else ring
    chips, _, width = mine_ref.shape
    units = gate_ref.shape[1]
    slots = ring.shape[0]
    ups = width // deep
    down_deep = min(deep, units)
    downs_k = units // down_deep
    halves = width // wide
    total = ups + halves * downs_k

    def up_copy(i):
        slot = lax.rem(i, slots)
        row = pl.multiple_of(i * deep, deep)
        return pltpu.make_async_copy(up_ref.at[pl.ds(row, deep)], ring.at[slot], sems.at[slot])

    def down_copy(i):
        slot = lax.rem(i, slots)
        j = i - ups
        row = pl.multiple_of(lax.rem(j, downs_k) * down_deep, down_deep)
        col = pl.multiple_of((j // downs_k) * wide, wide)
        return pltpu.make_async_copy(
            down_ref.at[pl.ds(row, down_deep), pl.ds(col, wide)],
            down_ring.at[slot],
            sems.at[slot],
        )

    def start(i):
        @pl.when(i < ups)
        def _():
            up_copy(i).start()

        @pl.when(jnp.logical_and(i >= ups, i < total))
        def _():
            down_copy(i).start()

    @pl.loop(0, min(slots, total))
    def _(i):
        start(i)

    join_rows(mine_ref, x_ref, 0)
    join_rows(other_ref, x_ref, chips * CAP)
    acc_a[...] = jnp.zeros_like(acc_a)
    acc_b[...] = jnp.zeros_like(acc_b)

    @pl.loop(0, ups, unroll=5)
    def _(i):
        row = pl.multiple_of(i * deep, deep)
        acc_a[...] += jnp.dot(
            x_ref[:, pl.ds(row, deep)],
            gate_ref[pl.ds(row, deep), :],
            preferred_element_type=jnp.float32,
        )

    @pl.loop(0, ups, unroll=5)
    def _(i):
        row = pl.multiple_of(i * deep, deep)
        up_copy(i).wait()
        acc_b[...] += jnp.dot(
            x_ref[:, pl.ds(row, deep)], ring[lax.rem(i, slots)], preferred_element_type=jnp.float32
        )
        start(i + slots)

    gate = acc_a[...]
    hid[...] = (gate / (1.0 + jnp.exp(-gate)) * acc_b[...]).astype(jnp.bfloat16)

    for half in range(halves):
        acc_c[...] = jnp.zeros_like(acc_c)

        @pl.loop(0, downs_k, unroll=downs_k)
        def _(k, half=half):
            i = ups + half * downs_k + k
            slot = lax.rem(i, slots)
            down_copy(i).wait()
            row = pl.multiple_of(k * down_deep, down_deep)
            acc_c[...] += jnp.dot(
                hid[:, pl.ds(row, down_deep)] if downs_k > 1 else hid[...],
                down_ring[slot],
                preferred_element_type=jnp.float32,
            )
            start(i + slots)

        for i in range(chips):
            for part_ref, first in ((own_ref, 0), (lent_ref, chips * CAP)):
                part_ref[i, :, half * wide : (half + 1) * wide] = acc_c[
                    first + i * CAP : first + (i + 1) * CAP, :
                ].astype(jnp.bfloat16)


def ffn(mine, other, gate, up, down):
    chips, _, width = mine.shape
    rows = 2 * chips * CAP
    units = gate.shape[1]
    deep, wide = DEEP, width // 2
    slots = 11 if rows <= 64 else 6
    down_deep = min(deep, units)
    rings = [pltpu.VMEM((slots, deep, units), jnp.bfloat16)]
    if (down_deep, wide) != (deep, units):
        rings.append(pltpu.VMEM((slots, down_deep, wide), jnp.bfloat16))
    vmem = pl.BlockSpec(memory_space=pltpu.VMEM)
    return pl.pallas_call(
        functools.partial(ffn_kernel, deep, wide),
        in_specs=[vmem] * 2 + [pl.BlockSpec(memory_space=pl.ANY)] * 2 + [vmem],
        out_specs=[vmem, vmem],
        out_shape=[blocks_out(mine.shape)] * 2,
        scratch_shapes=[
            pltpu.SemaphoreType.DMA((slots,)),
            pltpu.VMEM((rows, width), jnp.bfloat16),
            pltpu.VMEM((rows, units), jnp.float32),
            pltpu.VMEM((rows, units), jnp.float32),
            pltpu.VMEM((rows, wide), jnp.float32),
            pltpu.VMEM((rows, units), jnp.bfloat16),
            *rings,
        ],
        compiler_params=pltpu.CompilerParams(vmem_limit_bytes=(34 if rows <= 64 else 52) * MIB),
        cost_estimate=pl.CostEstimate(
            flops=6 * rows * width * units,
            bytes_accessed=4 * width * units,
            transcendentals=rows * units,
        ),
        name="ffn",
    )(
        blocks_in_vmem(mine),
        blocks_in_vmem(other),
        in_hbm(up),
        in_hbm(down),
        in_vmem(gate),
    )


def add_kernel(outers, inners, a_ref, b_ref, *outs):
    for i, ref, j in block_refs(outers, inners, outs):
        ref[j] = (a_ref[i].astype(jnp.float32) + b_ref[i].astype(jnp.float32)).astype(jnp.bfloat16)


def add(a, b):
    chips, _, width = a.shape
    outers, inners = grid_of(chips)
    vmem = pl.BlockSpec(memory_space=pltpu.VMEM)
    return pl.pallas_call(
        functools.partial(add_kernel, outers, inners),
        in_specs=[vmem] * 2,
        out_specs=[vmem] * (outers + inners - 1),
        out_shape=blocks_shapes(chips, width),
        compiler_params=pltpu.CompilerParams(vmem_limit_bytes=16 * MIB),
        name="add",
    )(blocks_in_vmem(a), blocks_in_vmem(b))


def unpack_kernel(outers, inners, target_ref, *refs):
    pieces, (out_ref, rows, out, sems) = refs[:-4], refs[-4:]
    chips = outers * inners
    index = lax.broadcasted_iota(jnp.int32, (rows.shape[0], 1), 0) // CAP
    layout = slot_layout(target_ref[...], partner_chips(chips, index) // (chips // EXP_FL))
    for i, block in piece_blocks(outers, inners, pieces):
        rows[i * CAP : (i + 1) * CAP, :] = block.astype(jnp.float32)
    count = sems.shape[0]
    part = rows.shape[1] // count
    moves = []
    for i in range(count):
        columns = slice(i * part, (i + 1) * part)
        out[:, columns] = lax.dot_general(
            layout,
            rows[:, columns].astype(jnp.bfloat16),
            (((0,), (0,)), ((), ())),
            preferred_element_type=jnp.float32,
        ).astype(jnp.bfloat16)
        moves.append(pltpu.make_async_copy(out.at[:, columns], out_ref.at[:, columns], sems.at[i]))
        moves[-1].start()
    for move in moves:
        move.wait()


def unpack(pieces, target, chips):
    width = pieces[0].shape[2]
    shape = (target.shape[1], width)
    return pl.pallas_call(
        functools.partial(unpack_kernel, *grid_of(chips)),
        in_specs=[pl.BlockSpec(memory_space=pltpu.VMEM)] * (1 + len(pieces)),
        out_specs=pl.BlockSpec(memory_space=pl.ANY),
        out_shape=jax.ShapeDtypeStruct(shape, jnp.bfloat16),
        scratch_shapes=[
            pltpu.VMEM((chips * CAP, width), jnp.float32),
            pltpu.VMEM(shape, jnp.bfloat16),
            pltpu.SemaphoreType.DMA((4,)),
        ],
        compiler_params=pltpu.CompilerParams(vmem_limit_bytes=(16 if chips <= 8 else 32) * MIB),
        name="unpack",
    )(in_vmem(target), *[blocks_in_vmem(x) for x in pieces])


def per_device(tokens, expert_ids, norm_gain, router, gate_weight, up_weight, down_weight):
    devices = lax.axis_size("expert")
    chips = devices // 2
    outers, inners = grid_of(chips)
    ids = expert_ids.reshape(1, -1)
    steps = [2 * inners * i for i in range(1, outers)]

    def send(x, offset):
        return lax.ppermute(x, "expert", [(i, i ^ offset) for i in range(devices)])

    def exchange(blocks):
        near = [send(x, 2 * (i + 1)) for i, x in enumerate(blocks[outers:])]
        direct = [send(x, step) for x, step in zip(blocks[1:outers], steps)]
        onward = [send(x, step) for x, step in zip(forward(near), steps[1:])]
        beside = [send(x, 2 * (i + 1)) for i, x in enumerate(forward(direct[:1]))]
        return [*onward, *beside, *direct[::-1], *near, blocks[0]]

    blocks, target = pack(tokens, ids, norm_gain.reshape(1, -1), router.T, up_weight, chips)
    mine = gather(exchange(blocks), chips)
    own, lent = ffn(mine, send(mine, 1), gate_weight, up_weight, down_weight)
    return unpack(exchange(add(own, send(lent, 1))), target, chips)


def solution(mesh):
    in_specs = (
        P(("groups", "expert"), None),
        P(("groups", "expert")),
        P(),
        P(),
        P(None, "expert"),
        P(None, "expert"),
        P("expert", None),
    )
    out_specs = P(("groups", "expert"), None)
    return jax.shard_map(
        per_device, mesh=mesh, in_specs=in_specs, out_specs=out_specs, check_vma=False
    )
```
